256 devices in a mesh: sub: 64 (over z, y, core), grp: 4 (over x).
Axes of the slice: x: 4, y: 4, z: 8, core: 2. Of those that a mesh axis runs over, the one named last changes fastest.
Arguments:
- schur_up: bfloat16 [2048, 384, 384], P(('sub', 'grp')), as said below
- schur_low: bfloat16 [2048, 384, 384], P(('sub', 'grp'))
- resid_up: bfloat16 [2048, 384, 128], P(('sub', 'grp')), may hold values from -6 to 6
- resid_low: bfloat16 [2048, 384, 128], P(('sub', 'grp')), may hold values from -6 to 6
- counts: int32 [256], P(('sub', 'grp')), may hold values from 1 to 8, as said below
- coarse_up: int32 [2048], P(('sub', 'grp')), may hold values from 0 to 2047, as said below
- coarse_low: int32 [2048], P(('sub', 'grp')), may hold values from 0 to 2047
Outputs:
- average_up: float32 [2048, 384, 128], P(('sub', 'grp'))
- average_low: float32 [2048, 384, 128], P(('sub', 'grp'))
- coarse: float32 [2048, 128], P(('sub', 'grp'))
The draws below stay inside these ranges and needn't reach their ends.
Inputs may be any that keep to these rules, and one draw needn't show every extreme that they name: counts lie between 1 and 8; counts of devices with the last sub index are not used. `coarse_up`: among the 8 upper and 8 lower slots of one device together, at most 2 name coarse unknowns of the same owner block (value // 8); every device has some owner block named exactly 2 times. `schur_up`: the two sides of a face have diagonals of one sign, of magnitude 2 to 3 each.
All inputs are finite; a program needn't handle non-finite values.
Results may differ from the reference program's by a relative error of at most 0.0003.
Values may be sent and summed in bfloat16 or wider, within the bound.
No kernel may reach another device: no remote copies, remote signals or barrier semaphores. Data moves between devices by JAX's collectives and lax.ppermute only.
A program may use at most 192 MiB of HBM per device.

```python
import jax
import jax.numpy as jnp
from jax import lax

F = 384
P_SIZE = 128
FC = 8
ITERS = 4
CO_DEV = 8
SLOTS = 2048
N_SUB = 64
N_GRP = 4
DEVICES = 256


def face_signs(key):
    sign_key = jax.random.fold_in(key, 101)
    coins = jax.random.randint(sign_key, (FC * DEVICES, F), 0, 2)
    return (2 * coins - 1).astype(jnp.float32)


def side_block(key, signs):
    magnitude_key, entry_key = jax.random.split(key)
    magnitude = jnp.exp(jax.random.uniform(magnitude_key, (FC * DEVICES, F), jnp.float32, jnp.log(2.0), jnp.log(3.0)))
    entries = jax.random.normal(entry_key, (FC * DEVICES, F, F), jnp.float32) * (1.8 / jnp.sqrt(jnp.float32(F)))
    identity = jnp.eye(F, dtype=jnp.float32)
    block = entries * (1.0 - identity)[None] + (signs * magnitude)[:, :, None] * identity[None]
    return block.astype(jnp.bfloat16)


def draw_schur_up(key, part):
    signs = face_signs(key)
    key = jax.random.fold_in(key, 3)
    return side_block(key, signs)


def draw_schur_low(key, part):
    signs = jnp.roll(face_signs(key), N_GRP * FC, axis=0)
    key = jax.random.fold_in(key, 5)
    return side_block(key, signs)


def draw_counts(key, part):
    key = jax.random.fold_in(key, 7)
    count_key, pick_key = jax.random.split(key)
    values = jax.random.randint(count_key, (DEVICES,), 1, FC + 1)
    chosen = jax.random.randint(pick_key, (), 0, DEVICES - N_GRP)
    return values.at[chosen].set(FC).astype(jnp.int32)


def device_targets(key, device):
    perm_key, step_key, order_key, local_key = jax.random.split(key, 4)
    offsets = jax.random.permutation(perm_key, DEVICES)[:2 * FC]
    steps = jax.random.randint(step_key, (2 * FC,), 0, 2)
    picks = jnp.arange(2 * FC, dtype=jnp.int32) - steps
    picks = jnp.where(jnp.arange(2 * FC, dtype=jnp.int32) < 2, 0, picks).astype(jnp.int32)
    order = jax.random.permutation(order_key, 2 * FC)
    owners = (device + offsets[picks[order]]) % DEVICES
    local = jax.random.randint(local_key, (2 * FC,), 0, CO_DEV)
    return (owners * CO_DEV + local).astype(jnp.int32)


def coarse_targets(key):
    base = jax.random.fold_in(key, 211)
    keys = jax.random.split(base, DEVICES)
    return jax.vmap(device_targets)(keys, jnp.arange(DEVICES, dtype=jnp.int32))


def draw_coarse_up(key, part):
    table = coarse_targets(key)
    return table[:, :FC].reshape(-1)


def draw_coarse_low(key, part):
    table = coarse_targets(key)
    return table[:, FC:].reshape(-1)


def block_levels(stream_key, dims, shards, smallest, high):
    factor_of = 1.0
    for dim, parts in shards:
        steps = jax.random.uniform(jax.random.fold_in(jax.random.fold_in(stream_key, 6), dim), (parts,), jnp.float32, smallest / len(shards), high / len(shards))
        factor_of = factor_of * jnp.repeat(jnp.exp(steps), dims[dim] // parts).reshape((-1,) + (1,) * (len(dims) - 1 - dim))
    return factor_of


def centred(key, shape, spread, bound, cuts=(), held_as=jnp.bfloat16):
    factor_of = block_levels(key, shape, cuts, -0.22, 0.18) if cuts else 1.0
    values = jax.random.normal(key, shape, jnp.float32) * spread * factor_of
    return jnp.minimum(jnp.maximum(values, -bound), bound).astype(held_as)


def setup_inputs(seed: int = 0) -> dict:
    splits = jax.random.split(jax.random.key(seed), 8)
    schur_up = draw_schur_up(jax.random.fold_in(splits[7], 71), 0)
    schur_low = draw_schur_low(jax.random.fold_in(splits[7], 71), 0)
    resid_up = centred(splits[2], (SLOTS, F, P_SIZE), 1.0, 6.0, ((0, 256),))
    resid_low = centred(splits[3], (SLOTS, F, P_SIZE), 1.0, 6.0, ((0, 256),))
    counts = draw_counts(jax.random.fold_in(splits[7], 71), 0)
    coarse_up = draw_coarse_up(jax.random.fold_in(splits[7], 71), 0)
    coarse_low = draw_coarse_low(jax.random.fold_in(splits[7], 71), 0)
    return {"schur_up": schur_up, "schur_low": schur_low, "resid_up": resid_up, "resid_low": resid_low, "counts": counts, "coarse_up": coarse_up, "coarse_low": coarse_low}


def solve_block(blocks):
    lower_side, upper_side, lower_rhs, upper_rhs = blocks
    lower_f = lower_side.astype(jnp.float32)
    upper_f = upper_side.astype(jnp.float32)
    matrix = lower_f + upper_f
    source = jnp.einsum('kab,kbp->kap', lower_f, lower_rhs.astype(jnp.float32), precision=lax.Precision.HIGHEST)
    source = source + jnp.einsum('kab,kbp->kap', upper_f, upper_rhs.astype(jnp.float32), precision=lax.Precision.HIGHEST)
    pivots = jnp.diagonal(matrix, axis1=1, axis2=2)[:, :, None]
    iterate = source / pivots
    for sweep in range(ITERS):
        product = jnp.einsum('kab,kbp->kap', matrix, iterate, precision=lax.Precision.HIGHEST)
        iterate = iterate + (source - product) / pivots
    return iterate

def side_flux(schur, resid, average, live):
    column_sums = lax.optimization_barrier(jnp.sum(schur.astype(jnp.float32), axis=1))
    diff = resid.astype(jnp.float32) - average
    flux = jnp.einsum('mf,mfp->mp', column_sums, diff, precision=lax.Precision.HIGHEST)
    return flux * (live[:, None] / jnp.sqrt(jnp.float32(F)))

def reference(schur_up, schur_low, resid_up, resid_low, counts, coarse_up, coarse_low):
    total = FC * N_SUB * N_GRP
    shift_rows = N_GRP * FC
    pairs = total - shift_rows
    slot_ids = jnp.arange(total, dtype=jnp.int32)
    device_ids = slot_ids // FC
    position = slot_ids % FC
    sub_ids = device_ids // N_GRP
    live_up = ((sub_ids < N_SUB - 1) & (position < counts[device_ids])).astype(jnp.float32)
    below = jnp.maximum(device_ids - N_GRP, 0).astype(jnp.int32)
    live_low = ((sub_ids > 0) & (position < counts[below])).astype(jnp.float32)
    blocks = pairs // FC
    lower_side = schur_up[:pairs].reshape(blocks, FC, F, F)
    upper_side = schur_low[shift_rows:].reshape(blocks, FC, F, F)
    lower_rhs = resid_up[:pairs].reshape(blocks, FC, F, P_SIZE)
    upper_rhs = resid_low[shift_rows:].reshape(blocks, FC, F, P_SIZE)
    solved = lax.map(solve_block, (lower_side, upper_side, lower_rhs, upper_rhs)).reshape(pairs, F, P_SIZE)
    solved = solved * live_up[:pairs][:, None, None]
    padding = jnp.zeros((shift_rows, F, P_SIZE), jnp.float32)
    average_up = jnp.concatenate([solved, padding], axis=0)
    average_low = jnp.concatenate([padding, solved], axis=0)
    flux_up = side_flux(schur_up, resid_up, average_up, live_up)
    flux_low = side_flux(schur_low, resid_low, average_low, live_low)
    fluxes = jnp.concatenate([flux_up, flux_low], axis=0)
    targets = jnp.concatenate([coarse_up, coarse_low], axis=0).astype(jnp.int32)
    coarse = jax.ops.segment_sum(fluxes, targets, num_segments=CO_DEV * N_SUB * N_GRP)
    return (average_up, average_low, coarse)
```

```python
import jax
import jax.numpy as jnp
from jax import lax
from jax.experimental import pallas as pl
from jax.experimental.pallas import tpu as pltpu
from jax.sharding import PartitionSpec as P

F = 384
COLS = 128
FC = 8
HALF = FC // 2
ITERS = 4
CO_DEV = 8
SLOTS = 4
BOTH = ("sub", "grp")


def swapped(value, odd):
    size = lax.axis_size("sub")
    pairs = []
    for i in range(size):
        j = ((i + 1) ^ 1) - 1 if odd else i ^ 1
        if 0 <= j < size:
            pairs.append((i, j))
    return lax.ppermute(value, "sub", pairs)


def split(value):
    high = value.astype(jnp.bfloat16)
    low = (value - high.astype(jnp.float32)).astype(jnp.bfloat16)
    return high, low


def mm(a, b):
    return jnp.dot(a, b, preferred_element_type=jnp.float32)


def three(row):
    high, low = split(row)
    rest = row - high.astype(jnp.float32) - low.astype(jnp.float32)
    return high.astype(jnp.float32), low.astype(jnp.float32), rest


def face_kernel(first, info, su, sl, ru, rl, other, x_out, flux_out):
    face = pl.program_id(0)
    use_up = info[0] == 1
    k = jnp.where(use_up, first, HALF + first) + face
    live = k < info[1]

    own_m = jnp.where(use_up, su[0], sl[0])
    own_r = jnp.where(use_up, ru[0], rl[0])
    oth_m = other[0, :, :F]
    oth_r = other[0, :, F:]

    source = mm(own_m, own_r) + mm(oth_m, oth_r)
    own_f = own_m.astype(jnp.float32)
    oth_f = oth_m.astype(jnp.float32)
    matrix = own_f + oth_f
    diagonal = lax.broadcasted_iota(jnp.int32, (F, F), 0) == lax.broadcasted_iota(
        jnp.int32, (F, F), 1
    )
    pivots = jnp.sum(jnp.where(diagonal, matrix, 0.0), axis=1, keepdims=True)
    inverse = 1.0 / pivots
    off_h, off_l = split(jnp.where(diagonal, 0.0, matrix))
    x = source * inverse
    for sweep in range(ITERS):
        x_h, x_l = split(x)
        wide = mm(off_h, jnp.concatenate([x_h, x_l], axis=1))
        product = wide[:, :COLS] + wide[:, COLS:] + mm(off_l, x_h)
        x = (source - product) * inverse
    x_out[0] = jnp.where(live, x, 0.0)

    sums_own = jnp.sum(own_f, axis=0, keepdims=True)
    sums_oth = jnp.sum(oth_f, axis=0, keepdims=True)
    rows = three(sums_own) + three(sums_oth)
    which = lax.broadcasted_iota(jnp.int32, (16, F), 0)
    left = jnp.zeros((16, F), jnp.float32)
    for i, row in enumerate(rows):
        left = jnp.where(which == i, row, left)
    x_h, x_l = split(x)
    right = jnp.concatenate([own_r, oth_r, x_h, x_l], axis=1)
    prod = mm(left.astype(jnp.bfloat16), right)
    moved = prod[:, 2 * COLS : 3 * COLS] + prod[:, 3 * COLS :]
    line = lax.broadcasted_iota(jnp.int32, (16, COLS), 0)
    own_flux = jnp.sum(jnp.where(line < 3, prod[:, :COLS] - moved, 0.0), axis=0, keepdims=True)
    oth_flux = jnp.sum(
        jnp.where((line >= 3) & (line < 6), prod[:, COLS : 2 * COLS] - moved, 0.0),
        axis=0,
        keepdims=True,
    )
    scale = 1.0 / jnp.sqrt(jnp.float32(F))
    row8 = lax.broadcasted_iota(jnp.int32, (8, COLS), 0)
    both = jnp.where(row8 == 0, own_flux, jnp.where(row8 == 1, oth_flux, 0.0)) * scale
    flux_out[0] = jnp.where(live, both, 0.0)


def solve_faces(info, first, count, su, sl, ru, rl, other):
    def up(i, s):
        return (jnp.where(s[0] == 1, first + i, first), 0, 0)

    def low(i, s):
        return (jnp.where(s[0] == 1, HALF + first, HALF + first + i), 0, 0)

    def kernel(*refs):
        face_kernel(first, *refs)

    return pl.pallas_call(
        kernel,
        grid_spec=pltpu.PrefetchScalarGridSpec(
            num_scalar_prefetch=1,
            grid=(count,),
            in_specs=[
                pl.BlockSpec((1, F, F), up),
                pl.BlockSpec((1, F, F), low),
                pl.BlockSpec((1, F, COLS), up),
                pl.BlockSpec((1, F, COLS), low),
                pl.BlockSpec((1, F, F + COLS), lambda i, s: (i, 0, 0)),
            ],
            out_specs=[
                pl.BlockSpec((1, F, COLS), lambda i, s: (i, 0, 0)),
                pl.BlockSpec((1, 8, COLS), lambda i, s: (i, 0, 0)),
            ],
        ),
        out_shape=[
            jax.ShapeDtypeStruct((count, F, COLS), jnp.float32),
            jax.ShapeDtypeStruct((count, 8, COLS), jnp.float32),
        ],
        compiler_params=pltpu.CompilerParams(vmem_limit_bytes=32 * 1024 * 1024),
        cost_estimate=pl.CostEstimate(
            flops=count * 14 * 2 * F * F * COLS, bytes_accessed=count * 1500000, transcendentals=0
        ),
    )(info, su, sl, ru, rl, other)


def shards(schur_up, schur_low, resid_up, resid_low, counts, coarse_up, coarse_low):
    subs = lax.axis_size("sub")
    devices = lax.axis_size(BOTH)
    s = lax.axis_index("sub")
    odd_core = s % 2 == 1

    def pick(if_odd, if_even):
        return jnp.where(odd_core, if_odd, if_even)

    def pack(lo, hi, use_up):
        up = jnp.concatenate([schur_up[HALF + lo : HALF + hi], resid_up[HALF + lo : HALF + hi]], 2)
        low = jnp.concatenate([schur_low[lo:hi], resid_low[lo:hi]], 2)
        return jnp.where(use_up, up, low)

    cut = HALF - 1
    got_a = swapped(pack(0, cut, odd_core), True)
    got_b = swapped(pack(cut, HALF, odd_core), True)
    got_e = swapped(pack(0, HALF, ~odd_core), False)
    below = lax.ppermute(counts, "sub", [(i, i + 1) for i in range(subs - 1)])
    their_target = swapped(pick(coarse_up[FC - 1], coarse_low[HALF - 1])[None], True)

    count_up = jnp.where(s < subs - 1, counts[0], 0)
    count_low = below[0]
    info_e = jnp.stack([pick(0, 1), pick(count_low, count_up)]).astype(jnp.int32)
    info_o = jnp.stack([pick(1, 0), pick(count_up, count_low)]).astype(jnp.int32)
    args = (schur_up, schur_low, resid_up, resid_low)

    x_e, flux_e = solve_faces(info_e, 0, HALF, *args, got_e)
    back_e, back_flux_e = swapped((x_e, flux_e[:, 1, :]), False)
    x_a, flux_a = solve_faces(info_o, 0, cut, *args, got_a)
    back_flux_a = swapped(flux_a[:, 1, :], True)
    x_b, flux_b = solve_faces(info_o, cut, 1, *args, got_b)
    x_o = jnp.concatenate([x_a, x_b], 0)
    back_o = swapped(x_o, True)

    rows = jnp.concatenate(
        [flux_e[:, 0], back_flux_e, flux_a[:, 0], flux_b[:, 0], back_flux_a, flux_b[:, 1]], 0
    )
    targets = jnp.concatenate(
        [
            pick(coarse_low[HALF:], coarse_up[:HALF]),
            pick(coarse_low[:HALF], coarse_up[HALF:]),
            pick(coarse_up[:HALF], coarse_low[HALF:]),
            pick(coarse_up[HALF : FC - 1], coarse_low[: HALF - 1]),
            their_target,
        ],
        0,
    )
    owner, local = targets // CO_DEV, targets % CO_DEV
    n = owner.shape[0]
    order = jnp.arange(n, dtype=jnp.int32)
    rank = jnp.sum(
        (owner[:, None] == owner[None, :]) & (order[None, :] < order[:, None]), axis=1
    ).astype(jnp.int32)
    heads = (jnp.arange(COLS)[None, :] == (rank * CO_DEV + local)[:, None]).astype(jnp.float32)
    places = jnp.concatenate([owner * SLOTS + rank, owner * SLOTS + SLOTS - 1], 0)
    chosen = (jnp.arange(devices * SLOTS)[:, None] == places[None, :]).astype(jnp.float32)
    parcels = jnp.dot(chosen, jnp.concatenate([rows, heads], 0), precision=lax.Precision.HIGHEST)
    arrived = lax.all_to_all(parcels.reshape(devices, SLOTS, COLS), BOTH, 0, 0, tiled=True)
    coarse = jnp.zeros((CO_DEV, COLS), jnp.float32)
    for r in range(SLOTS - 1):
        coarse = coarse + jnp.einsum(
            "dm,dp->mp",
            arrived[:, SLOTS - 1, r * CO_DEV : (r + 1) * CO_DEV],
            arrived[:, r, :],
            precision=lax.Precision.HIGHEST,
        )

    average_up = jnp.concatenate([pick(x_o, x_e), pick(back_o, back_e)], 0)
    average_low = jnp.concatenate([pick(back_e, back_o), pick(x_e, x_o)], 0)
    return (average_up, average_low, coarse)


def solution(mesh):
    return jax.shard_map(
        shards,
        mesh=mesh,
        in_specs=(
            P(BOTH, None, None),
            P(BOTH, None, None),
            P(BOTH, None, None),
            P(BOTH, None, None),
            P(BOTH),
            P(BOTH),
            P(BOTH),
        ),
        out_specs=(
            P(BOTH, None, None),
            P(BOTH, None, None),
            P(BOTH, None),
        ),
        check_vma=False,
    )
```

```python
import functools
import math

import jax
import jax.numpy as jnp
from jax import lax
from jax.experimental import pallas as pl
from jax.experimental.pallas import tpu as pltpu
from jax.sharding import PartitionSpec as P

F = 384
COLS = 128
WIDE = F + COLS
FC = 8
HALF = FC // 2
EARLY = 2
ITERS = 4
CO_DEV = 8
NOTE = 16
TAIL = 8
BOTH = ("sub", "grp")
BF, F32, I32 = jnp.bfloat16, jnp.float32, jnp.int32

ANY = pl.BlockSpec(memory_space=pl.ANY)
VM = pl.BlockSpec(memory_space=pltpu.VMEM)
SM = pl.BlockSpec(memory_space=pltpu.SMEM)
PARAMS = pltpu.CompilerParams(vmem_limit_bytes=16 * 1024 * 1024)


def vmem(shape, dtype):
    return pltpu.VMEM(shape, dtype)


def in_vmem(value):
    return pltpu.with_memory_space_constraint(value, pltpu.VMEM)


def in_hbm(value):
    return pltpu.with_memory_space_constraint(value, pltpu.HBM)


def swapped(value, odd):
    size = lax.axis_size("sub")
    pairs = []
    for i in range(size):
        j = ((i + 1) ^ 1) - 1 if odd else i ^ 1
        if 0 <= j < size:
            pairs.append((i, j))
    return lax.ppermute(value, "sub", pairs)


def load_kernel(plan, noted, info, su, sl, ru, rl, *rest):
    outs, sem = rest[-len(plan[1]) - 1 : -1], rest[-1]
    jobs, slot, place = [], 0, 0
    for kind, first, count, flag in plan[0]:
        use_up = info[flag] == 1
        for j in range(count):
            if kind == "pack":
                dst_m = outs[place].at[pl.ds(j * F, F), pl.ds(0, F)]
                dst_r = outs[place].at[pl.ds(j * F, F), pl.ds(F, COLS)]
                up, low = HALF + first + j, first + j
            else:
                dst_m, dst_r = outs[place].at[j], outs[place + 1].at[j]
                up, low = first + j, HALF + first + j
            jobs.append((use_up, up, low, dst_m, dst_r, slot))
            slot += 1
        place += 1 if kind == "pack" else 2
    for use_up, up, low, dst_m, dst_r, s in jobs:

        @pl.when(use_up)
        def _():
            pltpu.make_async_copy(su.at[up], dst_m, sem.at[0, s]).start()
            pltpu.make_async_copy(ru.at[up], dst_r, sem.at[1, s]).start()

        @pl.when(jnp.logical_not(use_up))
        def _():
            pltpu.make_async_copy(sl.at[low], dst_m, sem.at[0, s]).start()
            pltpu.make_async_copy(rl.at[low], dst_r, sem.at[1, s]).start()

    if noted:
        line = lax.broadcasted_iota(I32, (NOTE, WIDE), 0)
        note = jnp.zeros((NOTE, WIDE), I32)
        for i in range(1 + 2 * HALF):
            note = jnp.where(line == i, info[2 + i], note)
        rows = plan[0][0][2] * F
        outs[0][rows : rows + NOTE, :] = note.astype(F32).astype(BF)
    for use_up, up, low, dst_m, dst_r, s in jobs:
        pltpu.make_async_copy(su.at[up], dst_m, sem.at[0, s]).wait()
        pltpu.make_async_copy(ru.at[up], dst_r, sem.at[1, s]).wait()


def load(plan, noted, info, blocks, after=None):
    shapes, faces = [], 0
    for kind, first, count, flag in plan:
        faces += count
        if kind == "pack":
            extra = NOTE if noted and not shapes else 0
            shapes.append(vmem((count * F + extra, WIDE), BF))
        else:
            shapes += [vmem((count, F, F), BF), vmem((count, F, COLS), BF)]
    extra = [] if after is None else [in_vmem(after)]
    return pl.pallas_call(
        functools.partial(load_kernel, (plan, shapes), noted),
        in_specs=[SM] + [ANY] * (4 + len(extra)),
        out_specs=[VM] * len(shapes),
        out_shape=shapes,
        scratch_shapes=[pltpu.SemaphoreType.DMA((2, faces))],
        compiler_params=PARAMS,
    )(info, *[in_hbm(b) for b in blocks], *extra)


def split(value):
    high = value.astype(BF)
    return high, (value - high.astype(F32)).astype(BF)


def three(row):
    high, low = split(row)
    high, low = high.astype(F32), low.astype(F32)
    return high, low, row - high - low


def mm(a, b):
    return jnp.dot(a, b, preferred_element_type=F32)


def prepare(own_m, own_r, oth_m, oth_r):
    source = mm(own_m, own_r) + mm(oth_m, oth_r)
    own_f, oth_f = own_m.astype(F32), oth_m.astype(F32)
    sums = three(jnp.sum(own_f, axis=0, keepdims=True))
    sums += three(jnp.sum(oth_f, axis=0, keepdims=True))
    matrix = own_f + oth_f
    eye = lax.broadcasted_iota(I32, (128, 128), 0) == lax.broadcasted_iota(I32, (128, 128), 1)
    pivots, bands = [], []
    for b in range(F // 128):
        band = matrix[b * 128 : (b + 1) * 128]
        parts = [band[:, c * 128 : (c + 1) * 128] for c in range(F // 128)]
        pivots.append(jnp.sum(jnp.where(eye, parts[b], 0.0), axis=1, keepdims=True))
        parts[b] = jnp.where(eye, 0.0, parts[b])
        bands.append(jnp.concatenate(parts, 1))
    inverse = jnp.broadcast_to(1.0 / jnp.concatenate(pivots, 0), (F, COLS))
    high, low = split(jnp.concatenate(bands, 0))
    return source, inverse, high, low, sums


def sweep(x, state):
    source, inverse, high, low, _ = state
    x_h, x_l = split(x)
    wide = mm(high, jnp.concatenate([x_h, x_l], 1))
    return (source - (wide[:, :COLS] + wide[:, COLS:] + mm(low, x_h))) * inverse


def fluxes(x, own_r, oth_r, sums):
    line = lax.broadcasted_iota(I32, (16, F), 0)
    left = jnp.zeros((16, F), F32)
    for i, row in enumerate(sums):
        left = jnp.where(line == i, row, left)
    x_h, x_l = split(x)
    prod = mm(left.astype(BF), jnp.concatenate([own_r, oth_r, x_h, x_l], 1))[:8]
    moved = prod[:, 2 * COLS : 3 * COLS] + prod[:, 3 * COLS :]
    line = lax.broadcasted_iota(I32, (8, COLS), 0)
    scale = 1.0 / math.sqrt(F)
    own = jnp.where(line < 3, prod[:, :COLS] - moved, 0.0)
    oth = jnp.where((line >= 3) & (line < 6), prod[:, COLS : 2 * COLS] - moved, 0.0)
    return (
        jnp.sum(own, axis=0, keepdims=True) * scale,
        jnp.sum(oth, axis=0, keepdims=True) * scale,
    )


def solve_kernel(first, count, back, own_first, info, own_m, own_r, got, noted, *rest):
    x_out, flux_out = rest[-2:]
    use_up = info[0] == 1
    base = jnp.where(use_up, 0, HALF)
    rows = noted.shape[0] - NOTE
    told = noted[rows : rows + NOTE, :COLS].astype(F32)[:1]
    counts = jnp.where(info[1] == 1, info[2].astype(F32), told)
    flux_out[...] = jnp.zeros_like(flux_out)
    if back:
        x_out[HALF * F :, :] = jnp.zeros((TAIL, COLS), F32)
    for start in range(0, count, 2):
        faces = range(start, min(start + 2, count))
        others = [got[i * F : (i + 1) * F, :] for i in faces]
        states = [
            prepare(own_m[own_first + i], own_r[own_first + i], o[:, :F], o[:, F:])
            for i, o in zip(faces, others)
        ]
        xs = [s[0] * s[1] for s in states]
        for _ in range(ITERS):
            xs = [sweep(x, s) for x, s in zip(xs, states)]
        for i, x, s, o in zip(faces, xs, states, others):
            k = first + i
            live = (base + k).astype(F32) < counts
            x_out[k * F : (k + 1) * F, :] = jnp.where(live, x, 0.0)
            mine, theirs = fluxes(x, own_r[own_first + i], o[:, F:], s[4])
            flux_out[k : k + 1, :] = jnp.where(live, mine, 0.0)
            theirs = jnp.where(live, theirs, 0.0)
            if back:
                x_out[HALF * F + k : HALF * F + k + 1, :] = theirs
            else:
                flux_out[HALF + k : HALF + k + 1, :] = theirs


def solve(first, count, back, info, own_m, own_r, got, noted, after=(), into=None):
    args = [in_vmem(v) for v in (own_m, own_r, got, noted, *after)]
    alias = {}
    if into is not None:
        args.append(in_vmem(into))
        alias = {len(args): 0}
    return pl.pallas_call(
        functools.partial(solve_kernel, first, count, back, first),
        in_specs=[SM] + [VM] * len(args),
        out_specs=[VM, VM],
        out_shape=[vmem((HALF * F + (TAIL if back else 0), COLS), F32), vmem((2 * HALF, COLS), F32)],
        input_output_aliases=alias,
        compiler_params=PARAMS,
        cost_estimate=pl.CostEstimate(
            flops=count * 14 * 2 * F * F * COLS, bytes_accessed=count * 1000000, transcendentals=0
        ),
    )(info, *args)


SLOTS = 4


def encode_kernel(table, flux_e, back_e, flux_a, flux_b, out, codes, heads):
    rows = jnp.concatenate(
        [flux_e[:HALF], back_e[HALF * F : HALF * F + HALF, :], flux_a[...] + flux_b[...]], 0
    )
    top = jnp.max(jnp.abs(rows), axis=1, keepdims=True)
    step = jnp.broadcast_to(jnp.maximum(top, 1e-28) * (1.0 / 32767.0), rows.shape)
    power = jnp.clip(jnp.floor(jnp.log(step) * (1.0 / math.log(2.0))), -120.0, 120.0)
    unit = jnp.exp2(power)
    digits = jnp.round(step / unit * float(2**21))
    step = digits * unit * (2.0**-21)
    codes[...] = jnp.clip(jnp.round(rows / step), -32767.0, 32767.0).astype(I32)
    heads[...] = digits.astype(I32) * 256 + (power.astype(I32) + 128)
    out[...] = jnp.zeros_like(out)
    lane = lax.broadcasted_iota(I32, (1, COLS), 1)
    for i in range(4 * HALF):
        owner, rank, local, valid = table[0, i], table[1, i], table[2, i], table[3, i] == 1
        code = codes[i : i + 1, :]
        code = jnp.where(rank % 2 == 0, code * 65536, code & 65535)
        code = jnp.where(valid, code, 0)
        head = jnp.where((lane == rank * CO_DEV + local) & valid, heads[i : i + 1, :], 0)
        here = jnp.concatenate(
            [jnp.where(rank < 2, code, 0), jnp.where(rank >= 2, code, 0), head], 1
        )
        out[owner] = out[owner] | here


def encode(table, flux_e, back_e, flux_a, flux_b, devices):
    args = [in_vmem(v) for v in (flux_e, back_e, flux_a, flux_b)]
    return pl.pallas_call(
        encode_kernel,
        in_specs=[SM] + [VM] * 4,
        out_specs=VM,
        out_shape=vmem((devices, 1, 3 * COLS), I32),
        scratch_shapes=[pltpu.VMEM((4 * HALF, COLS), I32), pltpu.VMEM((4 * HALF, COLS), I32)],
        compiler_params=PARAMS,
    )(table, *args)


def decode_kernel(got, out):
    n = got.shape[0]
    words = [got[:, 0, c * COLS : (c + 1) * COLS] for c in range(3)]
    head = words[2]
    power = (head & 255).astype(F32) - 128.0
    step = jnp.where(head == 0, 0.0, (head >> 8).astype(F32) * (2.0**-21) * jnp.exp2(power))
    parts = []
    for w in words[:2]:
        for q in (w >> 16, (w << 16) >> 16):
            high = q >> 8
            parts.append((high.astype(F32) * 256.0).astype(BF))
            parts.append((q - high * 256).astype(F32).astype(BF))
    right = jnp.concatenate(parts, 1)
    total = jnp.zeros((CO_DEV, COLS), F32)
    prods = 0.0
    for piece in three(step):
        prods = prods + lax.dot_general(
            piece.astype(BF), right, (((0,), (0,)), ((), ())), preferred_element_type=F32
        )
    for r in range(SLOTS):
        rows = prods[r * CO_DEV : (r + 1) * CO_DEV]
        total = total + rows[:, 2 * r * COLS : (2 * r + 1) * COLS]
        total = total + rows[:, (2 * r + 1) * COLS : (2 * r + 2) * COLS]
    out[...] = total


def decode(arrived):
    return pl.pallas_call(
        decode_kernel,
        in_specs=[VM],
        out_specs=VM,
        out_shape=jax.ShapeDtypeStruct((CO_DEV, COLS), F32),
        compiler_params=PARAMS,
    )(in_vmem(arrived))


def shards(schur_up, schur_low, resid_up, resid_low, counts, coarse_up, coarse_low):
    subs = lax.axis_size("sub")
    devices = lax.axis_size(BOTH)
    s = lax.axis_index("sub")
    odd = (s % 2).astype(I32)
    even = 1 - odd
    blocks = (schur_up, schur_low, resid_up, resid_low)

    def pick(if_odd, if_even):
        return jnp.where(odd == 1, if_odd, if_even)

    sent = pick(coarse_up[HALF:], coarse_low[:HALF])
    info = jnp.concatenate([jnp.stack([odd, even]), counts, sent // 64, sent % 64]).astype(I32)

    (pack_a,) = load([("pack", 0, EARLY, 0)], True, info, blocks)
    got_a = swapped(pack_a, True)
    pack_e, own_e_m, own_e_r = load(
        [("pack", 0, HALF, 1), ("keep", 0, HALF, 1)], True, info, blocks, pack_a
    )
    got_e = swapped(pack_e, False)
    pack_b, own_o_m, own_o_r = load(
        [("pack", EARLY, HALF - EARLY, 0), ("keep", 0, HALF, 0)], False, info, blocks, pack_e
    )
    got_b = swapped(pack_b, True)

    count = jnp.where(s < subs - 1, counts[0], 0)
    info_e = jnp.stack([even, even, count])
    info_o = jnp.stack([odd, odd, count])

    x_e, flux_e = solve(0, HALF, True, info_e, own_e_m, own_e_r, got_e, got_e)
    back_e = swapped(x_e, False)
    x_a, flux_a = solve(0, EARLY, False, info_o, own_o_m, own_o_r, got_a, got_a, (flux_e,))
    x_o, flux_b = solve(
        EARLY, HALF - EARLY, False, info_o, own_o_m, own_o_r, got_b, got_a, (flux_a,), x_a
    )
    back_o = swapped(x_o, True)

    note = got_a[EARLY * F + 1 : EARLY * F + 1 + 2 * HALF, 0].astype(I32)
    theirs = note[:HALF] * 64 + note[HALF:]
    targets = jnp.concatenate(
        [
            pick(coarse_low[HALF:], coarse_up[:HALF]),
            pick(coarse_low[:HALF], coarse_up[HALF:]),
            pick(coarse_up[:HALF], coarse_low[HALF:]),
            theirs,
        ]
    )
    n = 4 * HALF
    order = jnp.arange(n, dtype=I32)
    paired = (order < n - HALF) | ((s > 0) & (s < subs - 1))
    owner, local = targets // CO_DEV, targets % CO_DEV
    same = (owner[:, None] == owner[None, :]) & (order[None, :] < order[:, None])
    rank = jnp.minimum(jnp.sum(same, axis=1), SLOTS - 1).astype(I32)
    table = jnp.stack([owner, rank, local, paired.astype(I32)])

    parcels = encode(table, flux_e, back_e, flux_a, flux_b, devices)
    arrived = lax.all_to_all(parcels, BOTH, 0, 0, tiled=True)
    coarse = decode(arrived)

    def panels(value):
        return value[: HALF * F].reshape(HALF, F, COLS)

    x_e, back_e, x_o, back_o = map(panels, (x_e, back_e, x_o, back_o))
    average_up = jnp.concatenate([pick(x_o, x_e), pick(back_o, back_e)], 0)
    average_low = jnp.concatenate([pick(back_e, back_o), pick(x_e, x_o)], 0)
    return (average_up, average_low, coarse)


def solution(mesh):
    return jax.shard_map(
        shards,
        mesh=mesh,
        in_specs=(
            P(BOTH, None, None),
            P(BOTH, None, None),
            P(BOTH, None, None),
            P(BOTH, None, None),
            P(BOTH),
            P(BOTH),
            P(BOTH),
        ),
        out_specs=(
            P(BOTH, None, None),
            P(BOTH, None, None),
            P(BOTH, None),
        ),
        check_vma=False,
    )
```

```python
import functools
import math

import jax
import jax.numpy as jnp
from jax import lax
from jax.experimental import pallas as pl
from jax.experimental.pallas import tpu as pltpu
from jax.sharding import PartitionSpec as P

F = 384
COLS = 128
WIDE = F + COLS
FC = 8
HALF = FC // 2
EARLY = 2
ITERS = 4
CO_DEV = 8
NOTE = 16
BOTH = ("sub", "grp")
BF, F32, I32, I16 = jnp.bfloat16, jnp.float32, jnp.int32, jnp.int16

ANY = pl.BlockSpec(memory_space=pl.ANY)
VM = pl.BlockSpec(memory_space=pltpu.VMEM)
SM = pl.BlockSpec(memory_space=pltpu.SMEM)
PARAMS = pltpu.CompilerParams(vmem_limit_bytes=10 * 1024 * 1024)


def vmem(shape, dtype):
    return pltpu.VMEM(shape, dtype)


def in_vmem(value):
    return pltpu.with_memory_space_constraint(value, pltpu.VMEM)


def in_hbm(value):
    return pltpu.with_memory_space_constraint(value, pltpu.HBM)


def swapped(value, odd):
    size = lax.axis_size("sub")
    pairs = []
    for i in range(size):
        j = ((i + 1) ^ 1) - 1 if odd else i ^ 1
        if 0 <= j < size:
            pairs.append((i, j))
    return lax.ppermute(value, "sub", pairs)


def pack_kernel(plans, *refs):
    su, sl, ru, rl = refs[:4]
    outs, (*small, note, sem) = refs[-4 - len(plans) : -4], refs[-4:]
    for i, (ref, kept_at) in enumerate(zip(refs[5:7], small)):
        pltpu.make_async_copy(ref, kept_at, sem.at[2, i]).start()
    odd = lax.rem(lax.axis_index("sub"), 2) == 1
    jobs = []
    for out, (first, count, across) in zip(outs, plans):
        for j in range(count):
            jobs.append((out, j, first + j, odd if across else jnp.logical_not(odd)))

    def copies(slot, out, j, m, r, face):
        return (
            pltpu.make_async_copy(m.at[face], out.at[pl.ds(j * F, F), pl.ds(0, F)], sem.at[0, slot]),
            pltpu.make_async_copy(r.at[face], out.at[pl.ds(j * F, F), pl.ds(F, COLS)], sem.at[1, slot]),
        )

    for slot, (out, j, face, use_up) in enumerate(jobs):

        @pl.when(use_up)
        def _():
            for c in copies(slot, out, j, su, ru, HALF + face):
                c.start()

        @pl.when(jnp.logical_not(use_up))
        def _():
            for c in copies(slot, out, j, sl, rl, face):
                c.start()

    for i, (ref, kept_at) in enumerate(zip(refs[5:7], small)):
        pltpu.make_async_copy(ref, kept_at, sem.at[2, i]).wait()
    coarse_up, coarse_low = small
    target = jnp.where(odd, coarse_up[:, HALF:], coarse_low[:, :HALF])
    note[...] = jnp.zeros_like(note)
    note[0:1, :] = jnp.broadcast_to(refs[4][0].astype(F32), (1, WIDE))
    note[1:2, :HALF] = (target // 64).astype(F32)
    note[2:3, :HALF] = (target % 64).astype(F32)
    rows = plans[0][1] * F
    outs[0][rows : rows + NOTE, :] = note[...].astype(BF)
    for slot, (out, j, face, _) in enumerate(jobs):
        for c in copies(slot, out, j, su, ru, HALF + face):
            c.wait()


def pack(plans, blocks, small, after=()):
    shapes = [vmem((count * F + (0 if i else NOTE), WIDE), BF) for i, (_, count, _) in enumerate(plans)]
    return pl.pallas_call(
        functools.partial(pack_kernel, plans),
        in_specs=[ANY] * 4 + [SM] + [ANY] * (2 + len(after)),
        out_specs=[VM] * len(shapes),
        out_shape=shapes,
        scratch_shapes=[
            vmem((1, FC), I32),
            vmem((1, FC), I32),
            vmem((NOTE, WIDE), F32),
            pltpu.SemaphoreType.DMA((3, FC)),
        ],
        compiler_params=PARAMS,
        cost_estimate=SMALL,
    )(*[in_hbm(b) for b in blocks], small[0], *[in_hbm(v[None]) for v in small[1:]], *after)


def split(value):
    high = value.astype(BF)
    return high, (value - high.astype(F32)).astype(BF)


def three(row):
    high, low = split(row)
    high, low = high.astype(F32), low.astype(F32)
    return high, low, row - high - low


def mm(a, b):
    return jnp.dot(a, b, preferred_element_type=F32)


def prepare(own_m, own_r, oth_m, oth_r):
    source = mm(own_m, own_r) + mm(oth_m, oth_r)
    own_f, oth_f = own_m.astype(F32), oth_m.astype(F32)
    sums = three(jnp.sum(own_f, axis=0, keepdims=True))
    sums += three(jnp.sum(oth_f, axis=0, keepdims=True))
    matrix = own_f + oth_f
    eye = lax.broadcasted_iota(I32, (128, 128), 0) == lax.broadcasted_iota(I32, (128, 128), 1)
    pivots, bands = [], []
    for b in range(F // 128):
        band = matrix[b * 128 : (b + 1) * 128]
        parts = [band[:, c * 128 : (c + 1) * 128] for c in range(F // 128)]
        pivots.append(jnp.sum(jnp.where(eye, parts[b], 0.0), axis=1, keepdims=True))
        parts[b] = jnp.where(eye, 0.0, parts[b])
        bands.append(jnp.concatenate(parts, 1))
    inverse = jnp.broadcast_to(1.0 / jnp.concatenate(pivots, 0), (F, COLS))
    high, low = split(jnp.concatenate(bands, 0))
    return source, inverse, high, low, sums


def sweep(x, state):
    source, inverse, high, low, _ = state
    x_h, x_l = split(x)
    wide = mm(high, jnp.concatenate([x_h, x_l], 1))
    return (source - (wide[:, :COLS] + wide[:, COLS:] + mm(low, x_h))) * inverse


def fluxes(x, own_r, oth_r, sums):
    line = lax.broadcasted_iota(I32, (16, F), 0)
    left = jnp.zeros((16, F), F32)
    for i, row in enumerate(sums):
        left = jnp.where(line == i, row, left)
    x_h, x_l = split(x)
    prod = mm(left.astype(BF), jnp.concatenate([own_r, oth_r, x_h, x_l], 1))[:8]
    moved = prod[:, 2 * COLS : 3 * COLS] + prod[:, 3 * COLS :]
    line = lax.broadcasted_iota(I32, (8, COLS), 0)
    scale = 1.0 / math.sqrt(F)
    own = jnp.where(line < 3, prod[:, :COLS] - moved, 0.0)
    oth = jnp.where((line >= 3) & (line < 6), prod[:, COLS : 2 * COLS] - moved, 0.0)
    return (
        jnp.sum(own, axis=0, keepdims=True) * scale,
        jnp.sum(oth, axis=0, keepdims=True) * scale,
    )


def solve_pair(own, others):
    states = [prepare(m, r, o[:, :F], o[:, F:]) for (m, r), o in zip(own, others)]
    xs = [s[0] * s[1] for s in states]
    for _ in range(ITERS):
        xs = [sweep(x, s) for x, s in zip(xs, states)]
    return [
        (x, *fluxes(x, r, o[:, F:], s[4])) for x, s, (_, r), o in zip(xs, states, own, others)
    ]


def keeper(su, sl, ru, rl, use_up, first, count, m, r, sem, row):
    def copies(i, sm, sr, face):
        return (
            pltpu.make_async_copy(sm.at[face], m.at[i], sem.at[row, i]),
            pltpu.make_async_copy(sr.at[face], r.at[i], sem.at[row + 1, i]),
        )

    def start(i):
        @pl.when(use_up)
        def _():
            for c in copies(i, su, ru, first + i):
                c.start()

        @pl.when(jnp.logical_not(use_up))
        def _():
            for c in copies(i, sl, rl, HALF + first + i):
                c.start()

    def wait(i):
        for c in copies(i, su, ru, first + i):
            c.wait()

    return start, wait


def count_of(lower, info, note):
    return jnp.where(lower, info[2].astype(F32), note.astype(F32)[:1])


def near_kernel(
    info, table, su, sl, ru, rl, got_1, got_2, x_out, flux_out, theirs_out, next_m, next_r, m, r, other, note, sem
):
    use_up = info[1] == 1
    own_start, own_wait = keeper(su, sl, ru, rl, use_up, 0, HALF, m, r, sem, 0)
    next_start, next_wait = keeper(
        su, sl, ru, rl, jnp.logical_not(use_up), 0, HALF, next_m, next_r, sem, 3
    )

    def got_copy(i):
        part, j = (got_1, i) if i < EARLY else (got_2, i - EARLY)
        return pltpu.make_async_copy(part.at[pl.ds(j * F, F)], other.at[i], sem.at[2, i])

    note_copy = pltpu.make_async_copy(got_1.at[pl.ds(EARLY * F, NOTE)], note, sem.at[2, HALF])
    for i in range(HALF):
        own_start(i)
        got_copy(i).start()
        if i == 0:
            note_copy.start()
    for i in range(HALF):
        next_start(i)
    flux_out[...] = jnp.zeros_like(flux_out)
    theirs_out[...] = jnp.zeros_like(theirs_out)
    base = jnp.where(use_up, 0, HALF)
    for start in range(0, HALF, 2):
        faces = (start, start + 1)
        for i in faces:
            own_wait(i)
            got_copy(i).wait()
        if start == 0:
            note_copy.wait()
            count = count_of(use_up, info, note[:, :COLS])
        solved = solve_pair([(m[i], r[i]) for i in faces], [other[i] for i in faces])
        for i, (x, mine, theirs) in zip(faces, solved):
            live = (base + i).astype(F32) < count
            x_out[i * F : (i + 1) * F, :] = jnp.where(live, x, 0.0)
            flux_out[i : i + 1, :] = jnp.where(live, mine, 0.0)
            theirs_out[i : i + 1, :] = jnp.where(live, theirs, 0.0)
    for i in range(HALF):
        next_wait(i)


def steps_of(top):
    step = jnp.maximum(top, 1e-28) * (1.0 / 32767.0)
    power = jnp.clip(jnp.floor(jnp.log(step) * (1.0 / math.log(2.0))), -120.0, 120.0)
    unit = jnp.exp2(power)
    digits = jnp.round(step / unit * float(2**21))
    return digits, power, digits * unit * (2.0**-21)


def coded(value, step):
    return jnp.clip(jnp.round(value / step), -32767.0, 32767.0).astype(I32)


def far_kernel(info, m, r, got, x_out, code_out, flux_out):
    use_up = info[0] == 1
    count = count_of(use_up, info, got[HALF * F : HALF * F + NOTE, :COLS])
    base = jnp.where(use_up, 0, HALF)
    line = lax.broadcasted_iota(I32, (NOTE, COLS), 0)
    tail = jnp.zeros((NOTE, COLS), I32)
    for start in range(0, HALF, 2):
        faces = (start, start + 1)
        solved = solve_pair(
            [(m[i], r[i]) for i in faces], [got[i * F : (i + 1) * F, :] for i in faces]
        )
        for i, (x, mine, theirs) in zip(faces, solved):
            live = (base + i).astype(F32) < count
            x = jnp.where(live, x, 0.0)
            x_out[i * F : (i + 1) * F, :] = x
            digits, power, step = steps_of(jnp.max(jnp.abs(x), axis=0, keepdims=True))
            code_out[i * F : (i + 1) * F, :] = coded(x, step).astype(I16)
            digits = digits.astype(I32)
            for j, row in enumerate((digits >> 11, digits & 2047, power.astype(I32))):
                tail = jnp.where(line == 3 * i + j, row, tail)
            flux_out[i : i + 1, :] = jnp.where(live, mine, 0.0)
            flux_out[HALF + i : HALF + i + 1, :] = jnp.where(live, theirs, 0.0)
    code_out[HALF * F :, :] = tail.astype(I16)


def kept(count):
    return [vmem((count, F, F), BF), vmem((count, F, COLS), BF)]


LARGE = pl.CostEstimate(flops=10**11, bytes_accessed=10**8, transcendentals=0)
SMALL = pl.CostEstimate(flops=1000, bytes_accessed=1000, transcendentals=0)


def solve_near(info, table, blocks, got_1, got_2):
    return pl.pallas_call(
        near_kernel,
        in_specs=[SM] * 2 + [ANY] * 6,
        out_specs=[VM] * 5,
        out_shape=[vmem((HALF * F, COLS), F32)] + [vmem((FC, COLS), F32)] * 2 + kept(HALF),
        scratch_shapes=[
            *kept(HALF),
            vmem((HALF, F, WIDE), BF),
            vmem((NOTE, WIDE), BF),
            pltpu.SemaphoreType.DMA((5, HALF + 1)),
        ],
        compiler_params=PARAMS,
        cost_estimate=SMALL,
    )(info, table, *[in_hbm(b) for b in blocks], in_hbm(got_1), in_hbm(got_2))


def solve_far(info, m, r, got):
    return pl.pallas_call(
        far_kernel,
        in_specs=[SM] + [VM] * 3,
        out_specs=[VM] * 3,
        out_shape=[
            vmem((HALF * F, COLS), F32),
            vmem((HALF * F + NOTE, COLS), I16),
            vmem((FC, COLS), F32),
        ],
        compiler_params=PARAMS,
        cost_estimate=SMALL,
    )(info, *map(in_vmem, (m, r, got)))


def place(ref, first, panels, sem, slot):
    out = []
    for i in range(HALF):
        c = pltpu.make_async_copy(panels.at[pl.ds(i * F, F)], ref.at[first + i], sem.at[slot, i])
        c.start()
        out.append(c)
    return out


def gather_kernel(x_e, back_e, x_o, up, low, sem):
    odd = lax.rem(lax.axis_index("sub"), 2) == 1

    @pl.when(odd)
    def _():
        copies = place(low, HALF, x_e, sem, 0) + place(low, 0, back_e, sem, 1)
        copies += place(up, 0, x_o, sem, 2)
        for c in copies:
            c.wait()

    @pl.when(jnp.logical_not(odd))
    def _():
        copies = place(up, 0, x_e, sem, 0) + place(up, HALF, back_e, sem, 1)
        copies += place(low, HALF, x_o, sem, 2)
        for c in copies:
            c.wait()


def gather(x_e, back_e, x_o):
    shape = pltpu.HBM((FC, F, COLS), F32)
    return pl.pallas_call(
        gather_kernel,
        in_specs=[VM] * 3,
        out_specs=[ANY] * 2,
        out_shape=[shape, shape],
        scratch_shapes=[pltpu.SemaphoreType.DMA((3, HALF))],
        compiler_params=PARAMS,
        cost_estimate=LARGE,
    )(x_e, back_e, x_o)


SLOTS = 4


def encode_kernel(table, flux_e, back_e, flux_o, got, out, codes, heads):
    rows = jnp.concatenate(
        [flux_e[:HALF], back_e[:HALF], flux_o[...]], 0
    )
    top = jnp.max(jnp.abs(rows), axis=1, keepdims=True)
    digits, power, step = steps_of(jnp.broadcast_to(top, rows.shape))
    codes[...] = coded(rows, step)
    heads[...] = digits.astype(I32) * 256 + (power.astype(I32) + 128)
    out[...] = jnp.zeros_like(out)
    lane = lax.broadcasted_iota(I32, (1, COLS), 1)
    none = jnp.zeros((1, COLS), I32)

    def place_row(i, owner, rank, local, far, valid):
        code = codes[i : i + 1, :]
        code = jnp.where(rank == 0, code * 65536, code & 65535)
        code = jnp.where(valid, code, 0)
        slot = rank + (2 if far else 0)
        head = jnp.where((lane == slot * CO_DEV + local) & valid, heads[i : i + 1, :], 0)
        out[owner] = out[owner] | jnp.concatenate(
            [none, code, head] if far else [code, none, head], 1
        )

    for i in range(3 * HALF):
        place_row(i, table[0, i], table[1, i], table[2, i], False, True)
    note = got[HALF * F : HALF * F + NOTE, :COLS].astype(F32)
    told = note[1:2] * 64.0 + note[2:3]
    owners = []
    for i in range(HALF):
        target = jnp.max(jnp.where(lane == i, told, 0.0)).astype(I32)
        owner = lax.div(target, CO_DEV)
        rank = 0
        for other in owners:
            rank = rank + jnp.where(other == owner, 1, 0)
        owners.append(owner)
        rank = jnp.minimum(rank, 1)
        place_row(3 * HALF + i, owner, rank, target - owner * CO_DEV, True, table[3, 0] == 1)


def encode(table, flux_e, back_e, flux_o, got, devices):
    return pl.pallas_call(
        encode_kernel,
        in_specs=[SM] + [VM] * 4,
        out_specs=VM,
        out_shape=vmem((devices, 1, 3 * COLS), I32),
        scratch_shapes=[vmem((4 * HALF, COLS), I32), vmem((4 * HALF, COLS), I32)],
        compiler_params=PARAMS,
        cost_estimate=SMALL,
    )(table, *map(in_vmem, (flux_e, back_e, flux_o, got)))


def decode(got):
    n = got.shape[0] // 3
    words = [got[pl.ds(c, n, stride=3), :] for c in range(3)]
    head = words[2]
    power = (head & 255).astype(F32) - 128.0
    step = jnp.where(head == 0, 0.0, (head >> 8).astype(F32) * (2.0**-21) * jnp.exp2(power))
    used = SLOTS * CO_DEV
    left = jnp.concatenate(three(step.T[:used]), 0).astype(BF)
    parts = []
    for w in words[:2]:
        for q in (w >> 16, (w << 16) >> 16):
            high = q >> 8
            parts.append((high.astype(F32) * 256.0).astype(BF))
            parts.append((q - high * 256).astype(F32).astype(BF))
    prods = mm(left, jnp.concatenate(parts, 1))
    prods = prods[:used] + prods[used : 2 * used] + prods[2 * used :]
    total = jnp.zeros((CO_DEV, COLS), F32)
    for r in range(SLOTS):
        rows = prods[r * CO_DEV : (r + 1) * CO_DEV]
        total = total + rows[:, 2 * r * COLS : (2 * r + 1) * COLS]
        total = total + rows[:, (2 * r + 1) * COLS : (2 * r + 2) * COLS]
    return total


def finish_kernel(arrived, back_o, up_in, low_in, up, low, coarse, panels, sem):
    odd = lax.rem(lax.axis_index("sub"), 2) == 1
    tail = back_o[HALF * F :, :].astype(I32)
    for i in range(HALF):
        high, rest, power = (tail[3 * i + j : 3 * i + j + 1] for j in range(3))
        step = (high * 2048 + rest).astype(F32) * jnp.exp2(power.astype(F32)) * (2.0**-21)
        panels[i] = back_o[i * F : (i + 1) * F, :].astype(I32).astype(F32) * step

        @pl.when(odd)
        def _():
            pltpu.make_async_copy(panels.at[i], up.at[HALF + i], sem.at[i]).start()

        @pl.when(jnp.logical_not(odd))
        def _():
            pltpu.make_async_copy(panels.at[i], low.at[i], sem.at[i]).start()

    coarse[...] = decode(arrived)
    for i in range(HALF):
        pltpu.make_async_copy(panels.at[i], up.at[HALF + i], sem.at[i]).wait()


def finish(arrived, back_o, up, low):
    shape = pltpu.HBM((FC, F, COLS), F32)
    return pl.pallas_call(
        finish_kernel,
        in_specs=[VM] * 2 + [ANY] * 2,
        out_specs=[ANY] * 2 + [VM],
        out_shape=[shape, shape, jax.ShapeDtypeStruct((CO_DEV, COLS), F32)],
        input_output_aliases={2: 0, 3: 1},
        scratch_shapes=[vmem((HALF, F, COLS), F32), pltpu.SemaphoreType.DMA((HALF,))],
        compiler_params=PARAMS,
    )(in_vmem(arrived), in_vmem(back_o), in_hbm(up), in_hbm(low))


def shards(schur_up, schur_low, resid_up, resid_low, counts, coarse_up, coarse_low):
    subs = lax.axis_size("sub")
    devices = lax.axis_size(BOTH)
    s = lax.axis_index("sub")
    odd = (s % 2).astype(I32)
    even = 1 - odd
    blocks = (schur_up, schur_low, resid_up, resid_low)

    def pick(if_odd, if_even):
        return jnp.where(odd == 1, if_odd, if_even)

    small = (counts, coarse_up, coarse_low)
    (pack_o,) = pack([(0, HALF, True)], blocks, small)
    got_o = swapped(pack_o, True)
    pack_1, pack_2 = pack(
        [(0, EARLY, False), (EARLY, HALF - EARLY, False)], blocks, small, (pack_o,)
    )
    got_1 = swapped(pack_1, False)
    got_2 = swapped(pack_2, False)

    count = jnp.where(s < subs - 1, counts[0], 0)
    info = jnp.stack([odd, even, count])
    targets = jnp.concatenate(
        [
            pick(coarse_low[HALF:], coarse_up[:HALF]),
            pick(coarse_low[:HALF], coarse_up[HALF:]),
            pick(coarse_up[:HALF], coarse_low[HALF:]),
        ]
    )
    order = jnp.arange(3 * HALF, dtype=I32)
    owner, local = targets // CO_DEV, targets % CO_DEV
    same = (owner[:, None] == owner[None, :]) & (order[None, :] < order[:, None])
    rank = jnp.minimum(jnp.sum(same, axis=1), 1).astype(I32)
    paired = jnp.broadcast_to(((s > 0) & (s < subs - 1)).astype(I32), owner.shape)
    table = jnp.stack([owner, rank, local, paired])

    x_e, flux_e, theirs_e, own_m, own_r = solve_near(info, table, blocks, got_1, got_2)
    back_e = swapped(x_e, False)
    back_flux = swapped(theirs_e, False)
    x_o, code_o, flux_o = solve_far(info, own_m, own_r, got_o)
    back_o = swapped(code_o, True)

    parcels = encode(table, flux_e, back_flux, flux_o, got_o, devices)
    arrived = lax.all_to_all(parcels, BOTH, 0, 0, tiled=True)
    up, low = gather(x_e, back_e, x_o)
    return finish(arrived.reshape(devices * 3, COLS), back_o, up, low)


def solution(mesh):
    return jax.shard_map(
        shards,
        mesh=mesh,
        in_specs=(
            P(BOTH, None, None),
            P(BOTH, None, None),
            P(BOTH, None, None),
            P(BOTH, None, None),
            P(BOTH),
            P(BOTH),
            P(BOTH),
        ),
        out_specs=(
            P(BOTH, None, None),
            P(BOTH, None, None),
            P(BOTH, None),
        ),
        check_vma=False,
    )
```

```python
import functools
import math

import jax
import jax.numpy as jnp
from jax import lax
from jax.experimental import pallas as pl
from jax.experimental.pallas import tpu as pltpu
from jax.sharding import PartitionSpec as P

F = 384
COLS = 128
WIDE = F + COLS
FC = 8
HALF = FC // 2
EARLY = 2
ITERS = 4
CO_DEV = 8
NOTE = 16
BOTH = ("sub", "grp")
BF, F32, I32, I16 = jnp.bfloat16, jnp.float32, jnp.int32, jnp.int16

ANY = pl.BlockSpec(memory_space=pl.ANY)
VM = pl.BlockSpec(memory_space=pltpu.VMEM)
SM = pl.BlockSpec(memory_space=pltpu.SMEM)
PARAMS = pltpu.CompilerParams(vmem_limit_bytes=10 * 1024 * 1024)


def vmem(shape, dtype):
    return pltpu.VMEM(shape, dtype)


def in_vmem(value):
    return pltpu.with_memory_space_constraint(value, pltpu.VMEM)


def in_hbm(value):
    return pltpu.with_memory_space_constraint(value, pltpu.HBM)


def swapped(value, odd):
    size = lax.axis_size("sub")
    pairs = []
    for i in range(size):
        j = ((i + 1) ^ 1) - 1 if odd else i ^ 1
        if 0 <= j < size:
            pairs.append((i, j))
    return lax.ppermute(value, "sub", pairs)


def pack_kernel(plans, *refs):
    su, sl, ru, rl = refs[:4]
    noted = any(plan[3] for plan in plans)
    outs, (*small, note, sem) = refs[-4 - len(plans) : -4], refs[-4:]
    if noted:
        for i, (ref, kept_at) in enumerate(zip(refs[5:7], small)):
            pltpu.make_async_copy(ref, kept_at, sem.at[2, i]).start()
    odd = lax.rem(lax.axis_index("sub"), 2) == 1
    jobs = []
    for out, (first, count, across, _) in zip(outs, plans):
        for j in range(count):
            jobs.append((out, j, first + j, odd if across else jnp.logical_not(odd)))

    def copies(slot, out, j, m, r, face):
        return (
            pltpu.make_async_copy(m.at[face], out.at[pl.ds(j * F, F), pl.ds(0, F)], sem.at[0, slot]),
            pltpu.make_async_copy(r.at[face], out.at[pl.ds(j * F, F), pl.ds(F, COLS)], sem.at[1, slot]),
        )

    for slot, (out, j, face, use_up) in enumerate(jobs):

        @pl.when(use_up)
        def _():
            for c in copies(slot, out, j, su, ru, HALF + face):
                c.start()

        @pl.when(jnp.logical_not(use_up))
        def _():
            for c in copies(slot, out, j, sl, rl, face):
                c.start()

    if noted:
        for i, (ref, kept_at) in enumerate(zip(refs[5:7], small)):
            pltpu.make_async_copy(ref, kept_at, sem.at[2, i]).wait()
        coarse_up, coarse_low = small
        target = jnp.where(odd, coarse_up[:, HALF:], coarse_low[:, :HALF])
        note[...] = jnp.zeros_like(note)
        note[0:1, :] = jnp.broadcast_to(refs[4][0].astype(F32), (1, WIDE))
        note[1:2, :HALF] = (target // 64).astype(F32)
        note[2:3, :HALF] = (target % 64).astype(F32)
        for out, plan in zip(outs, plans):
            if plan[3]:
                out[plan[1] * F : plan[1] * F + NOTE, :] = note[...].astype(BF)
    for slot, (out, j, face, _) in enumerate(jobs):
        for c in copies(slot, out, j, su, ru, HALF + face):
            c.wait()


def pack(plans, blocks, small=(), after=()):
    shapes = [vmem((plan[1] * F + (NOTE if plan[3] else 0), WIDE), BF) for plan in plans]
    given = [small[0], *[in_hbm(v[None]) for v in small[1:]]] if small else []
    return pl.pallas_call(
        functools.partial(pack_kernel, plans),
        in_specs=[ANY] * 4 + [SM] * len(small[:1]) + [ANY] * (len(small[1:]) + len(after)),
        out_specs=[VM] * len(shapes),
        out_shape=shapes,
        scratch_shapes=[
            vmem((1, FC), I32),
            vmem((1, FC), I32),
            vmem((NOTE, WIDE), F32),
            pltpu.SemaphoreType.DMA((3, FC)),
        ],
        compiler_params=PARAMS,
        cost_estimate=SMALL,
    )(*[in_hbm(b) for b in blocks], *given, *after)


def split(value):
    high = value.astype(BF)
    return high, (value - high.astype(F32)).astype(BF)


def three(row):
    high, low = split(row)
    high, low = high.astype(F32), low.astype(F32)
    return high, low, row - high - low


def mm(a, b):
    return jnp.dot(a, b, preferred_element_type=F32)


def prepare(own_m, own_r, oth_m, oth_r):
    source = mm(own_m, own_r) + mm(oth_m, oth_r)
    own_f, oth_f = own_m.astype(F32), oth_m.astype(F32)
    sums = three(jnp.sum(own_f, axis=0, keepdims=True))
    sums += three(jnp.sum(oth_f, axis=0, keepdims=True))
    matrix = own_f + oth_f
    eye = lax.broadcasted_iota(I32, (128, 128), 0) == lax.broadcasted_iota(I32, (128, 128), 1)
    pivots, bands = [], []
    for b in range(F // 128):
        band = matrix[b * 128 : (b + 1) * 128]
        parts = [band[:, c * 128 : (c + 1) * 128] for c in range(F // 128)]
        pivots.append(jnp.sum(jnp.where(eye, parts[b], 0.0), axis=1, keepdims=True))
        parts[b] = jnp.where(eye, 0.0, parts[b])
        bands.append(jnp.concatenate(parts, 1))
    inverse = jnp.broadcast_to(1.0 / jnp.concatenate(pivots, 0), (F, COLS))
    high, low = split(jnp.concatenate(bands, 0))
    return source, inverse, high, low, sums


def sweep(x, state):
    source, inverse, high, low, _ = state
    x_h, x_l = split(x)
    wide = mm(high, jnp.concatenate([x_h, x_l], 1))
    return (source - (wide[:, :COLS] + wide[:, COLS:] + mm(low, x_h))) * inverse


def fluxes(x, own_r, oth_r, sums):
    line = lax.broadcasted_iota(I32, (16, F), 0)
    left = jnp.zeros((16, F), F32)
    for i, row in enumerate(sums):
        left = jnp.where(line == i, row, left)
    x_h, x_l = split(x)
    prod = mm(left.astype(BF), jnp.concatenate([own_r, oth_r, x_h, x_l], 1))[:8]
    moved = prod[:, 2 * COLS : 3 * COLS] + prod[:, 3 * COLS :]
    line = lax.broadcasted_iota(I32, (8, COLS), 0)
    scale = 1.0 / math.sqrt(F)
    own = jnp.where(line < 3, prod[:, :COLS] - moved, 0.0)
    oth = jnp.where((line >= 3) & (line < 6), prod[:, COLS : 2 * COLS] - moved, 0.0)
    return (
        jnp.sum(own, axis=0, keepdims=True) * scale,
        jnp.sum(oth, axis=0, keepdims=True) * scale,
    )


def solve_pair(own, others):
    states = [prepare(m, r, o[:, :F], o[:, F:]) for (m, r), o in zip(own, others)]
    xs = [s[0] * s[1] for s in states]
    for _ in range(ITERS):
        xs = [sweep(x, s) for x, s in zip(xs, states)]
    return [
        (x, *fluxes(x, r, o[:, F:], s[4])) for x, s, (_, r), o in zip(xs, states, own, others)
    ]


def keeper(su, sl, ru, rl, use_up, first, count, m, r, sem, row):
    def copies(i, sm, sr, face):
        return (
            pltpu.make_async_copy(sm.at[face], m.at[i], sem.at[row, i]),
            pltpu.make_async_copy(sr.at[face], r.at[i], sem.at[row + 1, i]),
        )

    def start(i):
        @pl.when(use_up)
        def _():
            for c in copies(i, su, ru, first + i):
                c.start()

        @pl.when(jnp.logical_not(use_up))
        def _():
            for c in copies(i, sl, rl, HALF + first + i):
                c.start()

    def wait(i):
        for c in copies(i, su, ru, first + i):
            c.wait()

    return start, wait


def count_of(lower, info, note):
    return jnp.where(lower, info[2].astype(F32), note.astype(F32)[:1])


def near_kernel(
    info, table, su, sl, ru, rl, got_1, got_2, x_out, flux_out, theirs_out, next_m, next_r, m, r, other, note, sem
):
    use_up = info[1] == 1
    own_start, own_wait = keeper(su, sl, ru, rl, use_up, 0, HALF, m, r, sem, 0)
    next_start, next_wait = keeper(
        su, sl, ru, rl, jnp.logical_not(use_up), 0, HALF, next_m, next_r, sem, 3
    )

    def got_copy(i):
        part, j = (got_1, i) if i < 2 else (got_2, i - 2)
        return pltpu.make_async_copy(part.at[pl.ds(j * F, F)], other.at[i], sem.at[2, i])

    note_copy = pltpu.make_async_copy(got_1.at[pl.ds(2 * F, NOTE)], note, sem.at[2, HALF])
    for i in range(HALF):
        own_start(i)
        got_copy(i).start()
        if i == 0:
            note_copy.start()
    for i in range(HALF):
        next_start(i)
    flux_out[...] = jnp.zeros_like(flux_out)
    theirs_out[...] = jnp.zeros_like(theirs_out)
    base = jnp.where(use_up, 0, HALF)
    for start in range(0, HALF, 2):
        faces = (start, start + 1)
        for i in faces:
            own_wait(i)
            got_copy(i).wait()
        if start == 0:
            note_copy.wait()
            count = count_of(use_up, info, note[:, :COLS])
        solved = solve_pair([(m[i], r[i]) for i in faces], [other[i] for i in faces])
        for i, (x, mine, theirs) in zip(faces, solved):
            live = (base + i).astype(F32) < count
            x_out[i * F : (i + 1) * F, :] = jnp.where(live, x, 0.0)
            flux_out[i : i + 1, :] = jnp.where(live, mine, 0.0)
            theirs_out[i : i + 1, :] = jnp.where(live, theirs, 0.0)
    for i in range(HALF):
        next_wait(i)


def steps_of(top):
    step = jnp.maximum(top, 1e-28) * (1.0 / 32767.0)
    power = jnp.clip(jnp.floor(jnp.log(step) * (1.0 / math.log(2.0))), -120.0, 120.0)
    unit = jnp.exp2(power)
    digits = jnp.round(step / unit * float(2**21))
    return digits, power, digits * unit * (2.0**-21)


def coded(value, step):
    return jnp.clip(jnp.round(value / step), -32767.0, 32767.0).astype(I32)


def solve_all(first, count, m, r, got):
    out = []
    for start in range(0, count, 2):
        faces = range(start, min(start + 2, count))
        out += solve_pair(
            [(m[first + i], r[first + i]) for i in faces],
            [got[i * F : (i + 1) * F, :] for i in faces],
        )
    return out


def put_codes(x, ref, i, tail):
    digits, power, step = steps_of(jnp.max(jnp.abs(x), axis=0, keepdims=True))
    ref[i * F : (i + 1) * F, :] = coded(x, step).astype(I16)
    digits = digits.astype(I32)
    line = lax.broadcasted_iota(I32, tail.shape, 0)
    for j, row in enumerate((digits >> 11, digits & 2047, power.astype(I32))):
        tail = jnp.where(line == 3 * i + j, row, tail)
    return tail


def far_kernel(m, r, got, x_out, code_out, tail_out, flux_out):
    flux_out[...] = jnp.zeros_like(flux_out)
    tail = jnp.zeros((NOTE, COLS), I32)
    for i, (x, mine, theirs) in enumerate(solve_all(0, EARLY, m, r, got)):
        x_out[i * F : (i + 1) * F, :] = x
        tail = put_codes(x, code_out, i, tail)
        flux_out[i : i + 1, :] = mine
        flux_out[HALF + i : HALF + i + 1, :] = theirs
    tail_out[...] = tail


def last_kernel(info, m, r, got, x_in, code_in, tail_in, flux_in, x_out, code_out, flux_out):
    late = HALF - EARLY
    use_up = info[0] == 1
    count = count_of(use_up, info, got[late * F : late * F + NOTE, :COLS])
    base = jnp.where(use_up, 0, HALF)
    code_out[: EARLY * F, :] = code_in[...]
    tail = tail_in[...]
    solved = [
        (x_in[k * F : (k + 1) * F, :], flux_in[k : k + 1, :], flux_in[HALF + k : HALF + k + 1, :])
        for k in range(EARLY)
    ]
    solved += solve_all(EARLY, late, m, r, got)
    line = lax.broadcasted_iota(I32, (NOTE, COLS), 0)
    for i, (x, mine, theirs) in enumerate(solved):
        live = (base + i).astype(F32) < count
        x_out[i * F : (i + 1) * F, :] = jnp.where(live, x, 0.0)
        if i >= EARLY:
            tail = put_codes(x, code_out, i, tail)
        dead = jnp.logical_not(live)
        tail = jnp.where((line >= 3 * i) & (line < 3 * i + 3) & dead, 0, tail)
        flux_out[i : i + 1, :] = jnp.where(live, mine, 0.0)
        flux_out[HALF + i : HALF + i + 1, :] = jnp.where(live, theirs, 0.0)
    code_out[HALF * F :, :] = tail.astype(I16)


def kept(count):
    return [vmem((count, F, F), BF), vmem((count, F, COLS), BF)]


LARGE = pl.CostEstimate(flops=10**9, bytes_accessed=10**7, transcendentals=0)
SMALL = pl.CostEstimate(flops=1000, bytes_accessed=1000, transcendentals=0)


def solve_near(info, table, blocks, got_1, got_2):
    return pl.pallas_call(
        near_kernel,
        in_specs=[SM] * 2 + [ANY] * 6,
        out_specs=[VM] * 5,
        out_shape=[vmem((HALF * F, COLS), F32)] + [vmem((FC, COLS), F32)] * 2 + kept(HALF),
        scratch_shapes=[
            *kept(HALF),
            vmem((HALF, F, WIDE), BF),
            vmem((NOTE, WIDE), BF),
            pltpu.SemaphoreType.DMA((5, HALF + 1)),
        ],
        compiler_params=PARAMS,
        cost_estimate=SMALL,
    )(info, table, *[in_hbm(b) for b in blocks], in_hbm(got_1), in_hbm(got_2))


def solve_far(m, r, got):
    return pl.pallas_call(
        far_kernel,
        in_specs=[VM] * 3,
        out_specs=[VM] * 4,
        out_shape=[
            vmem((EARLY * F, COLS), F32),
            vmem((EARLY * F, COLS), I16),
            vmem((NOTE, COLS), I32),
            vmem((FC, COLS), F32),
        ],
        compiler_params=PARAMS,
        cost_estimate=SMALL,
    )(*map(in_vmem, (m, r, got)))


def solve_last(info, m, r, got, *early):
    return pl.pallas_call(
        last_kernel,
        in_specs=[SM] + [VM] * (3 + len(early)),
        out_specs=[VM] * 3,
        out_shape=[
            vmem((HALF * F, COLS), F32),
            vmem((HALF * F + NOTE, COLS), I16),
            vmem((FC, COLS), F32),
        ],
        compiler_params=PARAMS,
        cost_estimate=SMALL,
    )(info, *map(in_vmem, (m, r, got, *early)))


def place(ref, first, panels, sem, slot):
    out = []
    for i in range(HALF):
        c = pltpu.make_async_copy(panels.at[pl.ds(i * F, F)], ref.at[first + i], sem.at[slot, i])
        c.start()
        out.append(c)
    return out


def gather_kernel(x_e, back_e, x_o, up, low, sem):
    odd = lax.rem(lax.axis_index("sub"), 2) == 1

    @pl.when(odd)
    def _():
        copies = place(low, HALF, x_e, sem, 0) + place(low, 0, back_e, sem, 1)
        copies += place(up, 0, x_o, sem, 2)
        for c in copies:
            c.wait()

    @pl.when(jnp.logical_not(odd))
    def _():
        copies = place(up, 0, x_e, sem, 0) + place(up, HALF, back_e, sem, 1)
        copies += place(low, HALF, x_o, sem, 2)
        for c in copies:
            c.wait()


def gather(x_e, back_e, x_o):
    shape = pltpu.HBM((FC, F, COLS), F32)
    return pl.pallas_call(
        gather_kernel,
        in_specs=[VM] * 3,
        out_specs=[ANY] * 2,
        out_shape=[shape, shape],
        scratch_shapes=[pltpu.SemaphoreType.DMA((3, HALF))],
        compiler_params=PARAMS,
        cost_estimate=LARGE,
    )(x_e, back_e, x_o)


SLOTS = 4


def encode_kernel(table, flux_e, back_e, flux_o, got, out, codes, heads):
    rows = jnp.concatenate(
        [flux_e[:HALF], back_e[:HALF], flux_o[...]], 0
    )
    top = jnp.max(jnp.abs(rows), axis=1, keepdims=True)
    digits, power, step = steps_of(jnp.broadcast_to(top, rows.shape))
    codes[...] = coded(rows, step)
    heads[...] = digits.astype(I32) * 256 + (power.astype(I32) + 128)
    out[...] = jnp.zeros_like(out)
    lane = lax.broadcasted_iota(I32, (1, COLS), 1)
    none = jnp.zeros((1, COLS), I32)
    late = HALF - EARLY
    note = got[late * F : late * F + NOTE, :COLS].astype(F32)
    told = note[1:2] * 64.0 + note[2:3]
    rows = [(table[0, i], table[1, i], table[2, i]) for i in range(3 * HALF)]
    held = []
    for i in range(HALF):
        target = jnp.max(jnp.where(lane == i, told, 0.0)).astype(I32)
        owner = lax.div(target, CO_DEV)
        rank = 0
        for other in held:
            rank = rank + jnp.where(other == owner, 1, 0)
        held.append(owner)
        rows.append((owner, jnp.minimum(rank, 1), target - owner * CO_DEV))
    for i, (owner, rank, local) in enumerate(rows):
        far = i >= 3 * HALF
        code = codes[i : i + 1, :]
        code = jnp.where(rank == 0, code * 65536, code & 65535)
        slot = rank + (2 if far else 0)
        head = jnp.where(lane == slot * CO_DEV + local, heads[i : i + 1, :], 0)
        line = jnp.concatenate([none, code, head] if far else [code, none, head], 1)
        if far:
            line = jnp.where(table[3, 0] == 1, line, 0)
        out[owner] = out[owner] | line


def encode(table, flux_e, back_e, flux_o, got, devices):
    return pl.pallas_call(
        encode_kernel,
        in_specs=[SM] + [VM] * 4,
        out_specs=VM,
        out_shape=vmem((devices, 1, 3 * COLS), I32),
        scratch_shapes=[vmem((4 * HALF, COLS), I32)] * 2,
        compiler_params=PARAMS,
        cost_estimate=SMALL,
    )(table, *map(in_vmem, (flux_e, back_e, flux_o, got)))


def decode(got):
    n = got.shape[0] // 3
    words = [got[pl.ds(c, n, stride=3), :] for c in range(3)]
    head = words[2]
    power = (head & 255).astype(F32) - 128.0
    step = jnp.where(head == 0, 0.0, (head >> 8).astype(F32) * (2.0**-21) * jnp.exp2(power))
    used = SLOTS * CO_DEV
    left = jnp.concatenate(three(step.T[:used]), 0).astype(BF)
    parts = []
    for w in words[:2]:
        for q in (w >> 16, (w << 16) >> 16):
            high = q >> 8
            parts.append((high.astype(F32) * 256.0).astype(BF))
            parts.append((q - high * 256).astype(F32).astype(BF))
    prods = mm(left, jnp.concatenate(parts, 1))
    prods = prods[:used] + prods[used : 2 * used] + prods[2 * used :]
    total = jnp.zeros((CO_DEV, COLS), F32)
    for r in range(SLOTS):
        rows = prods[r * CO_DEV : (r + 1) * CO_DEV]
        total = total + rows[:, 2 * r * COLS : (2 * r + 1) * COLS]
        total = total + rows[:, (2 * r + 1) * COLS : (2 * r + 2) * COLS]
    return total


def panel_kernel(back_o, up_in, low_in, up, low, panels, sem):
    odd = lax.rem(lax.axis_index("sub"), 2) == 1
    tail = back_o[HALF * F :, :].astype(I32)
    for i in range(HALF):
        high, rest, power = (tail[3 * i + j : 3 * i + j + 1] for j in range(3))
        step = (high * 2048 + rest).astype(F32) * jnp.exp2(power.astype(F32)) * (2.0**-21)
        panels[i] = back_o[i * F : (i + 1) * F, :].astype(I32).astype(F32) * step

        @pl.when(odd)
        def _():
            pltpu.make_async_copy(panels.at[i], up.at[HALF + i], sem.at[i]).start()

        @pl.when(jnp.logical_not(odd))
        def _():
            pltpu.make_async_copy(panels.at[i], low.at[i], sem.at[i]).start()

    for i in range(HALF):
        pltpu.make_async_copy(panels.at[i], up.at[HALF + i], sem.at[i]).wait()


def put_panels(back_o, up, low):
    shape = pltpu.HBM((FC, F, COLS), F32)
    return pl.pallas_call(
        panel_kernel,
        in_specs=[VM] + [ANY] * 2,
        out_specs=[ANY] * 2,
        out_shape=[shape, shape],
        input_output_aliases={1: 0, 2: 1},
        scratch_shapes=[vmem((HALF, F, COLS), F32), pltpu.SemaphoreType.DMA((HALF,))],
        compiler_params=PARAMS,
        cost_estimate=SMALL,
    )(in_vmem(back_o), in_hbm(up), in_hbm(low))


def coarse_kernel(arrived, after, out):
    out[...] = decode(arrived)


def sum_rows(arrived, after):
    return pl.pallas_call(
        coarse_kernel,
        in_specs=[VM, ANY],
        out_specs=VM,
        out_shape=jax.ShapeDtypeStruct((CO_DEV, COLS), F32),
        compiler_params=PARAMS,
        cost_estimate=SMALL,
    )(in_vmem(arrived), in_hbm(after))


def shards(schur_up, schur_low, resid_up, resid_low, counts, coarse_up, coarse_low):
    subs = lax.axis_size("sub")
    devices = lax.axis_size(BOTH)
    s = lax.axis_index("sub")
    odd = (s % 2).astype(I32)
    even = 1 - odd
    blocks = (schur_up, schur_low, resid_up, resid_low)

    def pick(if_odd, if_even):
        return jnp.where(odd == 1, if_odd, if_even)

    (pack_a,) = pack([(0, EARLY, True, False)], blocks)
    got_a = swapped(pack_a, True)
    pack_1, pack_2, pack_b = pack(
        [(0, 2, False, True), (2, 2, False, False), (EARLY, HALF - EARLY, True, True)],
        blocks,
        (counts, coarse_up, coarse_low),
        (pack_a,),
    )
    got_1 = swapped(pack_1, False)
    got_2 = swapped(pack_2, False)
    got_b = swapped(pack_b, True)

    count = jnp.where(s < subs - 1, counts[0], 0)
    info = jnp.stack([odd, even, count])
    targets = jnp.concatenate(
        [
            pick(coarse_low[HALF:], coarse_up[:HALF]),
            pick(coarse_low[:HALF], coarse_up[HALF:]),
            pick(coarse_up[:HALF], coarse_low[HALF:]),
        ]
    )
    order = jnp.arange(3 * HALF, dtype=I32)
    owner, local = targets // CO_DEV, targets % CO_DEV
    same = (owner[:, None] == owner[None, :]) & (order[None, :] < order[:, None])
    rank = jnp.minimum(jnp.sum(same, axis=1), 1).astype(I32)
    paired = jnp.broadcast_to(((s > 0) & (s < subs - 1)).astype(I32), owner.shape)
    table = jnp.stack([owner, rank, local, paired])

    x_e, flux_e, theirs_e, own_m, own_r = solve_near(info, table, blocks, got_1, got_2)
    back_e = swapped(x_e, False)
    back_flux = swapped(theirs_e, False)
    early = solve_far(own_m, own_r, got_a)
    x_o, code_o, flux_o = solve_last(info, own_m, own_r, got_b, *early)
    back_o = swapped(code_o, True)

    parcels = encode(table, flux_e, back_flux, flux_o, got_b, devices)
    arrived = lax.all_to_all(parcels, BOTH, 0, 0, tiled=True)
    up, low = gather(x_e, back_e, x_o)
    up, low = put_panels(back_o, up, low)
    return (up, low, sum_rows(arrived.reshape(devices * 3, COLS), up))


def solution(mesh):
    return jax.shard_map(
        shards,
        mesh=mesh,
        in_specs=(
            P(BOTH, None, None),
            P(BOTH, None, None),
            P(BOTH, None, None),
            P(BOTH, None, None),
            P(BOTH),
            P(BOTH),
            P(BOTH),
        ),
        out_specs=(
            P(BOTH, None, None),
            P(BOTH, None, None),
            P(BOTH, None),
        ),
        check_vma=False,
    )
```

```python
import functools
import math

import jax
import jax.numpy as jnp
from jax import lax
from jax.experimental import pallas as pl
from jax.experimental.pallas import tpu as pltpu
from jax.sharding import PartitionSpec as P

F = 384
COLS = 128
WIDE = F + COLS
FC = 8
HALF = FC // 2
EARLY = 2
ITERS = 4
CO_DEV = 8
NOTE = 16
SUB = ("z", "y", "c")
ALL = (*SUB, "x")
ROWS = 4 * HALF
BF, F32, I32, I16 = jnp.bfloat16, jnp.float32, jnp.int32, jnp.int16

ANY = pl.BlockSpec(memory_space=pl.ANY)
VM = pl.BlockSpec(memory_space=pltpu.VMEM)
SM = pl.BlockSpec(memory_space=pltpu.SMEM)
PARAMS = pltpu.CompilerParams(vmem_limit_bytes=10 * 1024 * 1024)


def vmem(shape, dtype):
    return pltpu.VMEM(shape, dtype)


def in_vmem(value):
    return pltpu.with_memory_space_constraint(value, pltpu.VMEM)


def in_hbm(value):
    return pltpu.with_memory_space_constraint(value, pltpu.HBM)


def swapped(value, odd):
    size = lax.axis_size(SUB)
    pairs = []
    for i in range(size):
        j = ((i + 1) ^ 1) - 1 if odd else i ^ 1
        if 0 <= j < size:
            pairs.append((i, j))
    return lax.ppermute(value, SUB, pairs)


def pack_kernel(plans, *refs):
    su, sl, ru, rl = refs[:4]
    noted = any(plan[3] for plan in plans)
    outs, (*small, note, sem) = refs[-4 - len(plans) : -4], refs[-4:]
    if noted:
        for i, (ref, kept_at) in enumerate(zip(refs[5:7], small)):
            pltpu.make_async_copy(ref, kept_at, sem.at[2, i]).start()
    odd = lax.axis_index("c") == 1
    jobs = []
    for out, (first, count, across, _) in zip(outs, plans):
        for j in range(count):
            jobs.append((out, j, first + j, odd if across else jnp.logical_not(odd)))

    def copies(slot, out, j, m, r, face):
        return (
            pltpu.make_async_copy(m.at[face], out.at[pl.ds(j * F, F), pl.ds(0, F)], sem.at[0, slot]),
            pltpu.make_async_copy(r.at[face], out.at[pl.ds(j * F, F), pl.ds(F, COLS)], sem.at[1, slot]),
        )

    for slot, (out, j, face, use_up) in enumerate(jobs):

        @pl.when(use_up)
        def _():
            for c in copies(slot, out, j, su, ru, HALF + face):
                c.start()

        @pl.when(jnp.logical_not(use_up))
        def _():
            for c in copies(slot, out, j, sl, rl, face):
                c.start()

    if noted:
        for i, (ref, kept_at) in enumerate(zip(refs[5:7], small)):
            pltpu.make_async_copy(ref, kept_at, sem.at[2, i]).wait()
        coarse_up, coarse_low = small
        target = jnp.where(odd, coarse_up[:, HALF:], coarse_low[:, :HALF])
        note[...] = jnp.zeros_like(note)
        note[0:1, :] = jnp.broadcast_to(refs[4][0].astype(F32), (1, WIDE))
        note[1:2, 3 * HALF : ROWS] = (target // 64).astype(F32)
        note[2:3, 3 * HALF : ROWS] = (target % 64).astype(F32)
        for out, plan in zip(outs, plans):
            if plan[3]:
                out[plan[1] * F : plan[1] * F + NOTE, :] = note[...].astype(BF)
    for slot, (out, j, face, _) in enumerate(jobs):
        for c in copies(slot, out, j, su, ru, HALF + face):
            c.wait()


def pack(plans, blocks, small=(), after=()):
    shapes = [vmem((plan[1] * F + (NOTE if plan[3] else 0), WIDE), BF) for plan in plans]
    given = [small[0], *[in_hbm(v[None]) for v in small[1:]]] if small else []
    return pl.pallas_call(
        functools.partial(pack_kernel, plans),
        in_specs=[ANY] * 4 + [SM] * len(small[:1]) + [ANY] * (len(small[1:]) + len(after)),
        out_specs=[VM] * len(shapes),
        out_shape=shapes,
        scratch_shapes=[
            vmem((1, FC), I32),
            vmem((1, FC), I32),
            vmem((NOTE, WIDE), F32),
            pltpu.SemaphoreType.DMA((3, FC)),
        ],
        compiler_params=PARAMS,
        cost_estimate=SMALL,
    )(*[in_hbm(b) for b in blocks], *given, *after)


def split(value):
    high = value.astype(BF)
    return high, (value - high.astype(F32)).astype(BF)


def three(row):
    high, low = split(row)
    high, low = high.astype(F32), low.astype(F32)
    return high, low, row - high - low


def mm(a, b):
    return jnp.dot(a, b, preferred_element_type=F32)


def prepare(own_m, own_r, oth_m, oth_r):
    source = mm(own_m, own_r) + mm(oth_m, oth_r)
    own_f, oth_f = own_m.astype(F32), oth_m.astype(F32)
    sums = three(jnp.sum(own_f, axis=0, keepdims=True))
    sums += three(jnp.sum(oth_f, axis=0, keepdims=True))
    matrix = own_f + oth_f
    eye = lax.broadcasted_iota(I32, (128, 128), 0) == lax.broadcasted_iota(I32, (128, 128), 1)
    pivots, bands = [], []
    for b in range(F // 128):
        band = matrix[b * 128 : (b + 1) * 128]
        parts = [band[:, c * 128 : (c + 1) * 128] for c in range(F // 128)]
        pivots.append(jnp.sum(jnp.where(eye, parts[b], 0.0), axis=1, keepdims=True))
        parts[b] = jnp.where(eye, 0.0, parts[b])
        bands.append(jnp.concatenate(parts, 1))
    inverse = jnp.broadcast_to(1.0 / jnp.concatenate(pivots, 0), (F, COLS))
    high, low = split(jnp.concatenate(bands, 0))
    return source, inverse, high, low, sums


def sweep(x, state):
    source, inverse, high, low, _ = state
    x_h, x_l = split(x)
    wide = mm(high, jnp.concatenate([x_h, x_l], 1))
    return (source - (wide[:, :COLS] + wide[:, COLS:] + mm(low, x_h))) * inverse


def fluxes(x, own_r, oth_r, sums):
    line = lax.broadcasted_iota(I32, (16, F), 0)
    left = jnp.zeros((16, F), F32)
    for i, row in enumerate(sums):
        left = jnp.where(line == i, row, left)
    x_h, x_l = split(x)
    prod = mm(left.astype(BF), jnp.concatenate([own_r, oth_r, x_h, x_l], 1))[:8]
    moved = prod[:, 2 * COLS : 3 * COLS] + prod[:, 3 * COLS :]
    line = lax.broadcasted_iota(I32, (8, COLS), 0)
    scale = 1.0 / math.sqrt(F)
    own = jnp.where(line < 3, prod[:, :COLS] - moved, 0.0)
    oth = jnp.where((line >= 3) & (line < 6), prod[:, COLS : 2 * COLS] - moved, 0.0)
    return (
        jnp.sum(own, axis=0, keepdims=True) * scale,
        jnp.sum(oth, axis=0, keepdims=True) * scale,
    )


def solve_pair(own, others):
    states = [prepare(m, r, o[:, :F], o[:, F:]) for (m, r), o in zip(own, others)]
    xs = [s[0] * s[1] for s in states]
    for _ in range(ITERS):
        xs = [sweep(x, s) for x, s in zip(xs, states)]
    return [
        (x, *fluxes(x, r, o[:, F:], s[4])) for x, s, (_, r), o in zip(xs, states, own, others)
    ]


def keeper(su, sl, ru, rl, use_up, first, count, m, r, sem, row):
    def copies(i, sm, sr, face):
        return (
            pltpu.make_async_copy(sm.at[face], m.at[i], sem.at[row, i]),
            pltpu.make_async_copy(sr.at[face], r.at[i], sem.at[row + 1, i]),
        )

    def start(i):
        @pl.when(use_up)
        def _():
            for c in copies(i, su, ru, first + i):
                c.start()

        @pl.when(jnp.logical_not(use_up))
        def _():
            for c in copies(i, sl, rl, HALF + first + i):
                c.start()

    def wait(i):
        for c in copies(i, su, ru, first + i):
            c.wait()

    return start, wait


def count_of(lower, info, note):
    return jnp.where(lower, info[2].astype(F32), note.astype(F32)[:1])


def near_kernel(
    info, owned, su, sl, ru, rl, got_1, got_2, x_out, flux_out, theirs_out, next_m, next_r, m, r, other, note, sem
):
    use_up = info[1] == 1
    own_start, own_wait = keeper(su, sl, ru, rl, use_up, 0, HALF, m, r, sem, 0)
    next_start, next_wait = keeper(
        su, sl, ru, rl, jnp.logical_not(use_up), 0, HALF, next_m, next_r, sem, 3
    )

    def got_copy(i):
        part, j = (got_1, i) if i < 2 else (got_2, i - 2)
        return pltpu.make_async_copy(part.at[pl.ds(j * F, F)], other.at[i], sem.at[2, i])

    note_copy = pltpu.make_async_copy(got_1.at[pl.ds(2 * F, NOTE)], note, sem.at[2, HALF])
    for i in range(HALF):
        own_start(i)
        got_copy(i).start()
        if i == 0:
            note_copy.start()
    for i in range(HALF):
        next_start(i)
    flux_out[...] = jnp.zeros_like(flux_out)
    theirs_out[...] = jnp.zeros_like(theirs_out)
    base = jnp.where(use_up, 0, HALF)
    for start in range(0, HALF, 2):
        faces = (start, start + 1)
        for i in faces:
            own_wait(i)
            got_copy(i).wait()
        if start == 0:
            note_copy.wait()
            count = count_of(use_up, info, note[:, :COLS])
        solved = solve_pair([(m[i], r[i]) for i in faces], [other[i] for i in faces])
        for i, (x, mine, theirs) in zip(faces, solved):
            live = (base + i).astype(F32) < count
            x_out[i * F : (i + 1) * F, :] = jnp.where(live, x, 0.0)
            flux_out[i : i + 1, :] = jnp.where(live, mine, 0.0)
            theirs_out[i : i + 1, :] = jnp.where(live, theirs, 0.0)
    for i in range(HALF):
        next_wait(i)


def steps_of(top):
    step = jnp.maximum(top, 1e-28) * (1.0 / 32767.0)
    power = jnp.clip(jnp.floor(jnp.log(step) * (1.0 / math.log(2.0))), -120.0, 120.0)
    unit = jnp.exp2(power)
    digits = jnp.round(step / unit * float(2**21))
    return digits, power, digits * unit * (2.0**-21)


def coded(value, step):
    return jnp.clip(jnp.round(value / step), -32767.0, 32767.0).astype(I32)


def solve_all(first, count, m, r, got):
    out = []
    for start in range(0, count, 2):
        faces = range(start, min(start + 2, count))
        out += solve_pair(
            [(m[first + i], r[first + i]) for i in faces],
            [got[i * F : (i + 1) * F, :] for i in faces],
        )
    return out


def put_codes(x, ref, i, tail):
    digits, power, step = steps_of(jnp.max(jnp.abs(x), axis=0, keepdims=True))
    ref[i * F : (i + 1) * F, :] = coded(x, step).astype(I16)
    digits = digits.astype(I32)
    line = lax.broadcasted_iota(I32, tail.shape, 0)
    for j, row in enumerate((digits >> 11, digits & 2047, power.astype(I32))):
        tail = jnp.where(line == 3 * i + j, row, tail)
    return tail


def far_kernel(m, r, got, x_out, code_out, tail_out, flux_out):
    flux_out[...] = jnp.zeros_like(flux_out)
    tail = jnp.zeros((NOTE, COLS), I32)
    for i, (x, mine, theirs) in enumerate(solve_all(0, EARLY, m, r, got)):
        x_out[i * F : (i + 1) * F, :] = x
        tail = put_codes(x, code_out, i, tail)
        flux_out[i : i + 1, :] = mine
        flux_out[HALF + i : HALF + i + 1, :] = theirs
    tail_out[...] = tail


def last_kernel(
    info, m, r, got, x_in, code_in, tail_in, flux_in, after, x_out, code_out, flux_out
):
    late = HALF - EARLY
    use_up = info[0] == 1
    count = count_of(use_up, info, got[late * F : late * F + NOTE, :COLS])
    base = jnp.where(use_up, 0, HALF)
    code_out[: EARLY * F, :] = code_in[...]
    tail = tail_in[...]
    solved = [
        (x_in[k * F : (k + 1) * F, :], flux_in[k : k + 1, :], flux_in[HALF + k : HALF + k + 1, :])
        for k in range(EARLY)
    ]
    solved += solve_all(EARLY, late, m, r, got)
    line = lax.broadcasted_iota(I32, (NOTE, COLS), 0)
    for i, (x, mine, theirs) in enumerate(solved):
        live = (base + i).astype(F32) < count
        x_out[i * F : (i + 1) * F, :] = jnp.where(live, x, 0.0)
        if i >= EARLY:
            tail = put_codes(x, code_out, i, tail)
        dead = jnp.logical_not(live)
        tail = jnp.where((line >= 3 * i) & (line < 3 * i + 3) & dead, 0, tail)
        flux_out[i : i + 1, :] = jnp.where(live, mine, 0.0)
        flux_out[HALF + i : HALF + i + 1, :] = jnp.where(live, theirs, 0.0)
    code_out[HALF * F :, :] = tail.astype(I16)


def kept(count):
    return [vmem((count, F, F), BF), vmem((count, F, COLS), BF)]


SOME = pl.CostEstimate(flops=3*10**9, bytes_accessed=3*10**7, transcendentals=0)
SMALL = pl.CostEstimate(flops=1000, bytes_accessed=1000, transcendentals=0)


def passed_on(line):
    def kernel(line, out):
        out[...] = line[...]

    return pl.pallas_call(
        kernel,
        in_specs=[VM],
        out_specs=VM,
        out_shape=vmem(line.shape, line.dtype),
        compiler_params=PARAMS,
        cost_estimate=SOME,
    )(line)


def solve_near(info, owned, blocks, got_1, got_2):
    return pl.pallas_call(
        near_kernel,
        in_specs=[SM] + [ANY] * 7,
        out_specs=[VM] * 5,
        out_shape=[vmem((HALF * F, COLS), F32)] + [vmem((FC, COLS), F32)] * 2 + kept(HALF),
        scratch_shapes=[
            *kept(HALF),
            vmem((HALF, F, WIDE), BF),
            vmem((NOTE, WIDE), BF),
            pltpu.SemaphoreType.DMA((5, HALF + 1)),
        ],
        compiler_params=PARAMS,
        cost_estimate=SMALL,
    )(info, owned, *[in_hbm(b) for b in blocks], in_hbm(got_1), in_hbm(got_2))


def solve_far(m, r, got):
    return pl.pallas_call(
        far_kernel,
        in_specs=[VM] * 3,
        out_specs=[VM] * 4,
        out_shape=[
            vmem((EARLY * F, COLS), F32),
            vmem((EARLY * F, COLS), I16),
            vmem((NOTE, COLS), I32),
            vmem((FC, COLS), F32),
        ],
        compiler_params=PARAMS,
        cost_estimate=SMALL,
    )(*map(in_vmem, (m, r, got)))


def solve_last(info, m, r, got, *early):
    return pl.pallas_call(
        last_kernel,
        in_specs=[SM] + [VM] * (3 + len(early)),
        out_specs=[VM] * 3,
        out_shape=[
            vmem((HALF * F, COLS), F32),
            vmem((HALF * F + NOTE, COLS), I16),
            vmem((FC, COLS), F32),
        ],
        compiler_params=PARAMS,
        cost_estimate=SMALL,
    )(info, *map(in_vmem, (m, r, got, *early)))


def place(ref, first, panels, sem, slot):
    out = []
    for i in range(HALF):
        c = pltpu.make_async_copy(panels.at[pl.ds(i * F, F)], ref.at[first + i], sem.at[slot, i])
        c.start()
        out.append(c)
    return out


def gather_kernel(x_e, back_e, x_o, up, low, sem):
    odd = lax.axis_index("c") == 1

    @pl.when(odd)
    def _():
        copies = place(low, HALF, x_e, sem, 0) + place(low, 0, back_e, sem, 1)
        copies += place(up, 0, x_o, sem, 2)
        for c in copies:
            c.wait()

    @pl.when(jnp.logical_not(odd))
    def _():
        copies = place(up, 0, x_e, sem, 0) + place(up, HALF, back_e, sem, 1)
        copies += place(low, HALF, x_o, sem, 2)
        for c in copies:
            c.wait()


def gather(x_e, back_e, x_o):
    shape = pltpu.HBM((FC, F, COLS), F32)
    return pl.pallas_call(
        gather_kernel,
        in_specs=[VM] * 3,
        out_specs=[ANY] * 2,
        out_shape=[shape, shape],
        scratch_shapes=[pltpu.SemaphoreType.DMA((3, HALF))],
        compiler_params=PARAMS,
        cost_estimate=SOME,
    )(x_e, back_e, x_o)


def gather_rows_kernel(owned, flux_e, back_e, flux_o, got, out):
    rows = jnp.concatenate([flux_e[:HALF], back_e[:HALF], flux_o[...]], 0)
    top = jnp.max(jnp.abs(rows), axis=1, keepdims=True)
    digits, power, step = steps_of(jnp.broadcast_to(top, rows.shape))
    codes = coded(rows, step)
    scales = digits.astype(I32) * 256 + (power.astype(I32) + 128)
    late = HALF - EARLY
    note = got[late * F : late * F + NOTE, :COLS].astype(F32)
    head = (owned[...] + note[1:2] * 64.0 + note[2:3]).astype(I32)
    lane = lax.broadcasted_iota(I32, (1, COLS), 1)
    for i in range(ROWS):
        head = jnp.where(lane == ROWS + i, scales[i : i + 1], head)
    half = ROWS // 2
    pairs = codes[:half] * 65536 + (codes[half:] & 65535)
    line = jnp.concatenate([pairs[i : i + 1] for i in range(half)] + [head], 1)
    for d in range(out.shape[0]):
        out[d] = line


def gather_rows(owned, flux_e, back_e, flux_o, got, peers):
    return pl.pallas_call(
        gather_rows_kernel,
        in_specs=[VM] * 5,
        out_specs=VM,
        out_shape=vmem((peers, 1, (ROWS // 2 + 1) * COLS), I32),
        compiler_params=PARAMS,
        cost_estimate=SMALL,
    )(*map(in_vmem, (owned, flux_e, back_e, flux_o, got)))


def add_kernel(got, out):
    half = ROWS // 2
    peers = got.shape[0] // (half + 1)
    m = lax.broadcasted_iota(I32, (1, COLS), 1)
    wanted = (lax.axis_index("z") * 4 + (m >> 5)) * 2 + lax.axis_index("c")
    wanted = (wanted * 4 + ((m >> 3) & 3)) * CO_DEV + (m & 7)
    head = got[pl.ds(half, peers, stride=half + 1), :]
    step = (head >> 8).astype(F32) * jnp.exp2((head & 255).astype(F32) - 128.0) * (2.0**-21)
    words = [got[pl.ds(r, peers, stride=half + 1), :] for r in range(half)]
    codes = [w >> 16 for w in words] + [(w << 16) >> 16 for w in words]
    chosen, pieces = [], []
    for r in range(ROWS):
        target = jnp.broadcast_to(head[:, r : r + 1], (peers, COLS))
        chosen.append(jnp.where(target == wanted, 1.0, 0.0))
        pieces.append(codes[r].astype(F32) * step[:, ROWS + r : ROWS + r + 1])
    chosen = jnp.concatenate(chosen, 0).T.astype(BF)
    parts = [piece.astype(BF) for piece in three(jnp.concatenate(pieces, 0))]
    sums = mm(chosen, jnp.concatenate(parts, 1))
    sums = sums[:, :COLS] + sums[:, COLS : 2 * COLS] + sums[:, 2 * COLS :]
    for d in range(out.shape[0]):
        out[d] = sums[d * CO_DEV : (d + 1) * CO_DEV]


def add_rows(arrived, peers):
    return pl.pallas_call(
        add_kernel,
        in_specs=[VM],
        out_specs=VM,
        out_shape=vmem((peers, CO_DEV, COLS), F32),
        compiler_params=PARAMS,
        cost_estimate=SOME,
    )(in_vmem(arrived))


def panel_kernel(back_o, up_in, low_in, up, low, panels, sem):
    odd = lax.axis_index("c") == 1
    tail = back_o[HALF * F :, :].astype(I32)
    for i in range(HALF):
        high, rest, power = (tail[3 * i + j : 3 * i + j + 1] for j in range(3))
        step = (high * 2048 + rest).astype(F32) * jnp.exp2(power.astype(F32)) * (2.0**-21)
        panels[i] = back_o[i * F : (i + 1) * F, :].astype(I32).astype(F32) * step

        @pl.when(odd)
        def _():
            pltpu.make_async_copy(panels.at[i], up.at[HALF + i], sem.at[i]).start()

        @pl.when(jnp.logical_not(odd))
        def _():
            pltpu.make_async_copy(panels.at[i], low.at[i], sem.at[i]).start()

    for i in range(HALF):
        pltpu.make_async_copy(panels.at[i], up.at[HALF + i], sem.at[i]).wait()


def put_panels(back_o, up, low):
    shape = pltpu.HBM((FC, F, COLS), F32)
    return pl.pallas_call(
        panel_kernel,
        in_specs=[VM] + [ANY] * 2,
        out_specs=[ANY] * 2,
        out_shape=[shape, shape],
        input_output_aliases={1: 0, 2: 1},
        scratch_shapes=[vmem((HALF, F, COLS), F32), pltpu.SemaphoreType.DMA((HALF,))],
        compiler_params=PARAMS,
        cost_estimate=SMALL,
    )(in_vmem(back_o), in_hbm(up), in_hbm(low))


def coarse_kernel(arrived, after, out):
    total = arrived[0]
    for d in range(1, arrived.shape[0]):
        total = total + arrived[d]
    out[...] = total


def sum_rows(arrived, after):
    return pl.pallas_call(
        coarse_kernel,
        in_specs=[VM, ANY],
        out_specs=VM,
        out_shape=jax.ShapeDtypeStruct((CO_DEV, COLS), F32),
        compiler_params=PARAMS,
        cost_estimate=SMALL,
    )(in_vmem(arrived), in_hbm(after))


def shards(schur_up, schur_low, resid_up, resid_low, counts, coarse_up, coarse_low):
    subs = lax.axis_size(SUB)
    s = lax.axis_index(SUB)
    odd = lax.axis_index("c").astype(I32)
    even = 1 - odd
    blocks = (schur_up, schur_low, resid_up, resid_low)

    def pick(if_odd, if_even):
        return jnp.where(odd == 1, if_odd, if_even)

    (pack_a,) = pack([(0, EARLY, True, False)], blocks)
    got_a = swapped(pack_a, True)
    pack_1, pack_2, pack_b = pack(
        [(0, 2, False, True), (2, 2, False, False), (EARLY, HALF - EARLY, True, True)],
        blocks,
        (counts, coarse_up, coarse_low),
        (pack_a,),
    )
    got_1 = swapped(pack_1, False)
    got_2 = swapped(pack_2, False)
    got_b = swapped(pack_b, True)

    count = jnp.where(s < subs - 1, counts[0], 0)
    info = jnp.stack([odd, even, count])
    targets = jnp.concatenate(
        [
            pick(coarse_low[HALF:], coarse_up[:HALF]),
            pick(coarse_low[:HALF], coarse_up[HALF:]),
            pick(coarse_up[:HALF], coarse_low[HALF:]),
        ]
    )
    held = jnp.where((s > 0) & (s < subs - 1), 0, -1) * jnp.ones((HALF,), I32)
    owned = jnp.pad(jnp.concatenate([targets, held]), (0, COLS - ROWS)).astype(F32)[None]
    owned = passed_on(owned)

    x_e, flux_e, theirs_e, own_m, own_r = solve_near(info, owned, blocks, got_1, got_2)
    back_e = swapped(x_e, False)
    back_flux = swapped(theirs_e, False)
    early = solve_far(own_m, own_r, got_a)
    x_o, code_o, flux_o = solve_last(info, own_m, own_r, got_b, *early, back_flux)
    back_o = swapped(code_o, True)

    near_axes, far_axes = ("z", "c"), ("y", "x")
    peers = lax.axis_size(near_axes)
    parcels = gather_rows(owned, flux_e, back_flux, flux_o, got_b, peers)
    arrived = lax.all_to_all(parcels, near_axes, 0, 0, tiled=True)
    sums = add_rows(arrived.reshape(peers * (ROWS // 2 + 1), COLS), lax.axis_size(far_axes))
    sums = lax.all_to_all(sums, far_axes, 0, 0, tiled=True)
    up, low = gather(x_e, back_e, x_o)
    up, low = put_panels(back_o, up, low)
    return (up, low, sum_rows(sums, up))


def solution(mesh):
    devices = mesh.devices.reshape(-1, 4, 2, mesh.shape["grp"])
    return jax.shard_map(
        shards,
        mesh=jax.sharding.Mesh(devices, ALL),
        in_specs=(
            P(ALL, None, None),
            P(ALL, None, None),
            P(ALL, None, None),
            P(ALL, None, None),
            P(ALL),
            P(ALL),
            P(ALL),
        ),
        out_specs=(
            P(ALL, None, None),
            P(ALL, None, None),
            P(ALL, None),
        ),
        check_vma=False,
    )
```

```python
import functools
import math

import jax
import jax.numpy as jnp
from jax import lax
from jax.experimental import pallas as pl
from jax.experimental.pallas import tpu as pltpu
from jax.sharding import PartitionSpec as P

F = 384
COLS = 128
WIDE = F + COLS
FC = 8
HALF = FC // 2
EARLY = 3
ITERS = 4
CO_DEV = 8
NOTE = 16
SUB = ("z", "y", "c")
ALL = (*SUB, "x")
ROWS = 4 * HALF
BF, F32, I32, I16 = jnp.bfloat16, jnp.float32, jnp.int32, jnp.int16

ANY = pl.BlockSpec(memory_space=pl.ANY)
VM = pl.BlockSpec(memory_space=pltpu.VMEM)
SM = pl.BlockSpec(memory_space=pltpu.SMEM)
PARAMS = pltpu.CompilerParams(vmem_limit_bytes=10 * 1024 * 1024)


def vmem(shape, dtype):
    return pltpu.VMEM(shape, dtype)


def in_vmem(value):
    return pltpu.with_memory_space_constraint(value, pltpu.VMEM)


def in_hbm(value):
    return pltpu.with_memory_space_constraint(value, pltpu.HBM)


def swapped(value, odd):
    size = lax.axis_size(SUB)
    pairs = []
    for i in range(size):
        j = ((i + 1) ^ 1) - 1 if odd else i ^ 1
        if 0 <= j < size:
            pairs.append((i, j))
    return lax.ppermute(value, SUB, pairs)


def pack_kernel(plans, *refs):
    su, sl, ru, rl = refs[:4]
    noted = any(plan[3] for plan in plans)
    outs, (*small, note, sem) = refs[-4 - len(plans) - noted : -4], refs[-4:]
    if noted:
        for i, (ref, kept_at) in enumerate(zip(refs[5:7], small)):
            pltpu.make_async_copy(ref, kept_at, sem.at[2, i]).start()
    odd = lax.axis_index("c") == 1
    jobs = []
    for out, (first, count, across, _) in zip(outs, plans):
        for j in range(count):
            jobs.append((out, j, first + j, odd if across else jnp.logical_not(odd)))

    def copies(slot, out, j, m, r, face):
        return (
            pltpu.make_async_copy(m.at[face], out.at[pl.ds(j * F, F), pl.ds(0, F)], sem.at[0, slot]),
            pltpu.make_async_copy(r.at[face], out.at[pl.ds(j * F, F), pl.ds(F, COLS)], sem.at[1, slot]),
        )

    for slot, (out, j, face, use_up) in enumerate(jobs):

        @pl.when(use_up)
        def _():
            for c in copies(slot, out, j, su, ru, HALF + face):
                c.start()

        @pl.when(jnp.logical_not(use_up))
        def _():
            for c in copies(slot, out, j, sl, rl, face):
                c.start()

    if noted:
        for i, (ref, kept_at) in enumerate(zip(refs[5:7], small)):
            pltpu.make_async_copy(ref, kept_at, sem.at[2, i]).wait()
        coarse_up, coarse_low = small
        target = jnp.where(odd, coarse_up[:, HALF:], coarse_low[:, :HALF])
        note[...] = jnp.zeros_like(note)
        note[0:1, :] = jnp.broadcast_to(refs[4][0].astype(F32), (1, WIDE))
        note[1:2, 3 * HALF : ROWS] = (target // 64).astype(F32)
        note[2:3, 3 * HALF : ROWS] = (target % 64).astype(F32)
        for out, plan in zip(outs, plans):
            for k in range(plan[3]):
                start = plan[1] * F + k * NOTE
                out[start : start + NOTE, :] = note[...].astype(BF)
        owned = outs[-1]
        s = (lax.axis_index("z") * 4 + lax.axis_index("y")) * 2 + lax.axis_index("c")
        alone = (s == 0) | (s == lax.axis_size(SUB) - 1)
        owned[...] = jnp.zeros_like(owned)
        parts = [
            jnp.where(odd, coarse_low[:, HALF:], coarse_up[:, :HALF]),
            jnp.where(odd, coarse_low[:, :HALF], coarse_up[:, HALF:]),
            jnp.where(odd, coarse_up[:, :HALF], coarse_low[:, HALF:]),
            jnp.broadcast_to(jnp.where(alone, -1, 0), (1, HALF)),
        ]
        for i, part in enumerate(parts):
            owned[:, i * HALF : (i + 1) * HALF] = part.astype(F32)
    for slot, (out, j, face, _) in enumerate(jobs):
        for c in copies(slot, out, j, su, ru, HALF + face):
            c.wait()


def pack(plans, blocks, small=(), after=()):
    shapes = [vmem((plan[1] * F + NOTE * plan[3], WIDE), BF) for plan in plans]
    if small:
        shapes.append(jax.ShapeDtypeStruct((1, COLS), F32))
    given = [small[0], *[in_hbm(v[None]) for v in small[1:]]] if small else []
    return pl.pallas_call(
        functools.partial(pack_kernel, plans),
        in_specs=[ANY] * 4 + [SM] * len(small[:1]) + [ANY] * (len(small[1:]) + len(after)),
        out_specs=[VM] * len(shapes),
        out_shape=shapes,
        scratch_shapes=[
            vmem((1, FC), I32),
            vmem((1, FC), I32),
            vmem((NOTE, WIDE), F32),
            pltpu.SemaphoreType.DMA((3, FC)),
        ],
        compiler_params=PARAMS,
        cost_estimate=SMALL,
    )(*[in_hbm(b) for b in blocks], *given, *after)


def split(value):
    high = value.astype(BF)
    return high, (value - high.astype(F32)).astype(BF)


def three(row):
    high, low = split(row)
    high, low = high.astype(F32), low.astype(F32)
    return high, low, row - high - low


def mm(a, b):
    return jnp.dot(a, b, preferred_element_type=F32)


def prepare(own_m, own_r, oth_m, oth_r):
    source = mm(own_m, own_r) + mm(oth_m, oth_r)
    own_f, oth_f = own_m.astype(F32), oth_m.astype(F32)
    sums = three(jnp.sum(own_f, axis=0, keepdims=True))
    sums += three(jnp.sum(oth_f, axis=0, keepdims=True))
    matrix = own_f + oth_f
    eye = lax.broadcasted_iota(I32, (128, 128), 0) == lax.broadcasted_iota(I32, (128, 128), 1)
    pivots, bands = [], []
    for b in range(F // 128):
        band = matrix[b * 128 : (b + 1) * 128]
        parts = [band[:, c * 128 : (c + 1) * 128] for c in range(F // 128)]
        pivots.append(jnp.sum(jnp.where(eye, parts[b], 0.0), axis=1, keepdims=True))
        parts[b] = jnp.where(eye, 0.0, parts[b])
        bands.append(jnp.concatenate(parts, 1))
    inverse = jnp.broadcast_to(1.0 / jnp.concatenate(pivots, 0), (F, COLS))
    high, low = split(jnp.concatenate(bands, 0))
    return source, inverse, high, low, sums


def sweep(x, state):
    source, inverse, high, low, _ = state
    x_h, x_l = split(x)
    wide = mm(high, jnp.concatenate([x_h, x_l], 1))
    return (source - (wide[:, :COLS] + wide[:, COLS:] + mm(low, x_h))) * inverse


def fluxes(x, own_r, oth_r, sums):
    line = lax.broadcasted_iota(I32, (16, F), 0)
    left = jnp.zeros((16, F), F32)
    for i, row in enumerate(sums):
        left = jnp.where(line == i, row, left)
    x_h, x_l = split(x)
    prod = mm(left.astype(BF), jnp.concatenate([own_r, oth_r, x_h, x_l], 1))[:8]
    moved = prod[:, 2 * COLS : 3 * COLS] + prod[:, 3 * COLS :]
    line = lax.broadcasted_iota(I32, (8, COLS), 0)
    scale = 1.0 / math.sqrt(F)
    own = jnp.where(line < 3, prod[:, :COLS] - moved, 0.0)
    oth = jnp.where((line >= 3) & (line < 6), prod[:, COLS : 2 * COLS] - moved, 0.0)
    return (
        jnp.sum(own, axis=0, keepdims=True) * scale,
        jnp.sum(oth, axis=0, keepdims=True) * scale,
    )


def solve_pair(own, others):
    states = [prepare(m, r, o[:, :F], o[:, F:]) for (m, r), o in zip(own, others)]
    xs = [s[0] * s[1] for s in states]
    for _ in range(ITERS):
        xs = [sweep(x, s) for x, s in zip(xs, states)]
    return [
        (x, *fluxes(x, r, o[:, F:], s[4])) for x, s, (_, r), o in zip(xs, states, own, others)
    ]


def keeper(su, sl, ru, rl, use_up, first, count, m, r, sem, row):
    def copies(i, sm, sr, face):
        return (
            pltpu.make_async_copy(sm.at[face], m.at[i], sem.at[row, i]),
            pltpu.make_async_copy(sr.at[face], r.at[i], sem.at[row + 1, i]),
        )

    def start(i):
        @pl.when(use_up)
        def _():
            for c in copies(i, su, ru, first + i):
                c.start()

        @pl.when(jnp.logical_not(use_up))
        def _():
            for c in copies(i, sl, rl, HALF + first + i):
                c.start()

    def wait(i):
        for c in copies(i, su, ru, first + i):
            c.wait()

    return start, wait


def count_of(lower, info, note):
    return jnp.where(lower, info[2].astype(F32), note.astype(F32)[:1])


def near_kernel(info, after, su, sl, ru, rl, *refs):
    got = refs[:HALF]
    x_out, flux_out, theirs_out, next_m, next_r, m, r, other, note, sem = refs[HALF:]
    use_up = info[1] == 1
    own_start, own_wait = keeper(su, sl, ru, rl, use_up, 0, HALF, m, r, sem, 0)
    next_start, next_wait = keeper(
        su, sl, ru, rl, jnp.logical_not(use_up), 0, HALF, next_m, next_r, sem, 3
    )

    def got_copy(i):
        return pltpu.make_async_copy(got[i].at[pl.ds(0, F)], other.at[i], sem.at[2, i])

    note_copy = pltpu.make_async_copy(got[0].at[pl.ds(F, NOTE)], note, sem.at[2, HALF])
    for i in range(HALF):
        own_start(i)
        got_copy(i).start()
        if i == 0:
            note_copy.start()
    flux_out[...] = jnp.zeros_like(flux_out)
    theirs_out[...] = jnp.zeros_like(theirs_out)
    base = jnp.where(use_up, 0, HALF)
    for start in range(0, HALF, 2):
        faces = (start, start + 1)
        for i in faces:
            own_wait(i)
            got_copy(i).wait()
        if start == 0:
            for i in range(HALF):
                next_start(i)
            note_copy.wait()
            count = count_of(use_up, info, note[:, :COLS])
        solved = solve_pair([(m[i], r[i]) for i in faces], [other[i] for i in faces])
        for i, (x, mine, theirs) in zip(faces, solved):
            live = (base + i).astype(F32) < count
            x_out[i * F : (i + 1) * F, :] = jnp.where(live, x, 0.0)
            flux_out[i : i + 1, :] = jnp.where(live, mine, 0.0)
            theirs_out[i : i + 1, :] = jnp.where(live, theirs, 0.0)
    for i in range(HALF):
        next_wait(i)


def steps_of(top):
    step = jnp.maximum(top, 1e-28) * (1.0 / 32767.0)
    power = jnp.clip(jnp.floor(jnp.log(step) * (1.0 / math.log(2.0))), -120.0, 120.0)
    unit = jnp.exp2(power)
    digits = jnp.round(step / unit * float(2**21))
    return digits, power, digits * unit * (2.0**-21)


def coded(value, step):
    return jnp.clip(jnp.round(value / step), -32767.0, 32767.0).astype(I32)


def solve_all(first, count, m, r, got):
    out = []
    for start in range(0, count, 3):
        faces = range(start, min(start + 3, count))
        out += solve_pair(
            [(m[first + i], r[first + i]) for i in faces],
            [got[i * F : (i + 1) * F, :] for i in faces],
        )
    return out


def put_codes(x, ref, i, tail):
    digits, power, step = steps_of(jnp.max(jnp.abs(x), axis=0, keepdims=True))
    ref[i * F : (i + 1) * F, :] = coded(x, step).astype(I16)
    digits = digits.astype(I32)
    line = lax.broadcasted_iota(I32, tail.shape, 0)
    for j, row in enumerate((digits >> 11, digits & 2047, power.astype(I32))):
        tail = jnp.where(line == 3 * i + j, row, tail)
    return tail


def far_kernel(m, r, got, x_out, code_out, tail_out, flux_out):
    flux_out[...] = jnp.zeros_like(flux_out)
    tail = jnp.zeros((NOTE, COLS), I32)
    for i, (x, mine, theirs) in enumerate(solve_all(0, EARLY, m, r, got)):
        x_out[i * F : (i + 1) * F, :] = x
        tail = put_codes(x, code_out, i, tail)
        flux_out[i : i + 1, :] = mine
        flux_out[HALF + i : HALF + i + 1, :] = theirs
    tail_out[...] = tail


def last_kernel(
    info, m, r, got, x_in, code_in, tail_in, flux_in, after, x_out, code_out, flux_out
):
    late = HALF - EARLY
    use_up = info[0] == 1
    count = count_of(use_up, info, got[late * F : late * F + NOTE, :COLS])
    base = jnp.where(use_up, 0, HALF)
    code_out[: EARLY * F, :] = code_in[...]
    tail = tail_in[...]
    solved = [
        (x_in[k * F : (k + 1) * F, :], flux_in[k : k + 1, :], flux_in[HALF + k : HALF + k + 1, :])
        for k in range(EARLY)
    ]
    solved += solve_all(EARLY, late, m, r, got)
    line = lax.broadcasted_iota(I32, (NOTE, COLS), 0)
    for i, (x, mine, theirs) in enumerate(solved):
        live = (base + i).astype(F32) < count
        x_out[i * F : (i + 1) * F, :] = jnp.where(live, x, 0.0)
        if i >= EARLY:
            tail = put_codes(x, code_out, i, tail)
        dead = jnp.logical_not(live)
        tail = jnp.where((line >= 3 * i) & (line < 3 * i + 3) & dead, 0, tail)
        flux_out[i : i + 1, :] = jnp.where(live, mine, 0.0)
        flux_out[HALF + i : HALF + i + 1, :] = jnp.where(live, theirs, 0.0)
    code_out[HALF * F :, :] = tail.astype(I16)


def kept(count):
    return [vmem((count, F, F), BF), vmem((count, F, COLS), BF)]


SOME = pl.CostEstimate(flops=3*10**9, bytes_accessed=3*10**7, transcendentals=0)
SMALL = pl.CostEstimate(flops=1000, bytes_accessed=1000, transcendentals=0)


def passed_on(value):
    def kernel(value, out):
        out[...] = value[...]

    return pl.pallas_call(
        kernel,
        in_specs=[VM],
        out_specs=VM,
        out_shape=vmem(value.shape, value.dtype),
        compiler_params=PARAMS,
        cost_estimate=SOME,
    )(in_vmem(value))


def solve_near(info, after, blocks, got_near):
    return pl.pallas_call(
        near_kernel,
        in_specs=[SM] + [ANY] * (5 + HALF),
        out_specs=[VM] * 5,
        out_shape=[vmem((HALF * F, COLS), F32)] + [vmem((FC, COLS), F32)] * 2 + kept(HALF),
        scratch_shapes=[
            *kept(HALF),
            vmem((HALF, F, WIDE), BF),
            vmem((NOTE, WIDE), BF),
            pltpu.SemaphoreType.DMA((5, HALF + 1)),
        ],
        compiler_params=PARAMS,
        cost_estimate=SMALL,
    )(info, after, *[in_hbm(b) for b in (*blocks, *got_near)])


def solve_far(m, r, got):
    return pl.pallas_call(
        far_kernel,
        in_specs=[VM] * 3,
        out_specs=[VM] * 4,
        out_shape=[
            vmem((EARLY * F, COLS), F32),
            vmem((EARLY * F, COLS), I16),
            vmem((NOTE, COLS), I32),
            vmem((FC, COLS), F32),
        ],
        compiler_params=PARAMS,
        cost_estimate=SMALL,
    )(*map(in_vmem, (m, r, got)))


def solve_last(info, m, r, got, *early):
    return pl.pallas_call(
        last_kernel,
        in_specs=[SM] + [VM] * (3 + len(early)),
        out_specs=[VM] * 3,
        out_shape=[
            vmem((HALF * F, COLS), F32),
            vmem((HALF * F + NOTE, COLS), I16),
            vmem((FC, COLS), F32),
        ],
        compiler_params=PARAMS,
        cost_estimate=SMALL,
    )(info, *map(in_vmem, (m, r, got, *early)))


def place(ref, first, panels, sem, slot):
    out = []
    for i in range(HALF):
        c = pltpu.make_async_copy(panels.at[pl.ds(i * F, F)], ref.at[first + i], sem.at[slot, i])
        c.start()
        out.append(c)
    return out


def gather_kernel(x_e, back_e, x_o, up, low, sem):
    odd = lax.axis_index("c") == 1

    @pl.when(odd)
    def _():
        copies = place(low, HALF, x_e, sem, 0) + place(low, 0, back_e, sem, 1)
        copies += place(up, 0, x_o, sem, 2)
        for c in copies:
            c.wait()

    @pl.when(jnp.logical_not(odd))
    def _():
        copies = place(up, 0, x_e, sem, 0) + place(up, HALF, back_e, sem, 1)
        copies += place(low, HALF, x_o, sem, 2)
        for c in copies:
            c.wait()


def gather(x_e, back_e, x_o):
    shape = pltpu.HBM((FC, F, COLS), F32)
    return pl.pallas_call(
        gather_kernel,
        in_specs=[VM] * 3,
        out_specs=[ANY] * 2,
        out_shape=[shape, shape],
        scratch_shapes=[pltpu.SemaphoreType.DMA((3, HALF))],
        compiler_params=PARAMS,
        cost_estimate=SOME,
    )(x_e, back_e, x_o)


def gather_rows_kernel(owned, flux_e, back_e, flux_o, got, out):
    rows = jnp.concatenate([flux_e[:HALF], back_e[:HALF], flux_o[...]], 0)
    top = jnp.max(jnp.abs(rows), axis=1, keepdims=True)
    digits, power, step = steps_of(jnp.broadcast_to(top, rows.shape))
    codes = coded(rows, step)
    scales = digits.astype(I32) * 256 + (power.astype(I32) + 128)
    late = HALF - EARLY
    note = got[late * F : late * F + NOTE, :COLS].astype(F32)
    head = (owned[...] + note[1:2] * 64.0 + note[2:3]).astype(I32)
    lane = lax.broadcasted_iota(I32, (1, COLS), 1)
    for i in range(ROWS):
        head = jnp.where(lane == ROWS + i, scales[i : i + 1], head)
    half = ROWS // 2
    pairs = codes[:half] * 65536 + (codes[half:] & 65535)
    line = jnp.concatenate([pairs[i : i + 1] for i in range(half)] + [head], 1)
    for d in range(out.shape[0]):
        out[d] = line


def gather_rows(owned, flux_e, back_e, flux_o, got, peers):
    return pl.pallas_call(
        gather_rows_kernel,
        in_specs=[VM] * 5,
        out_specs=VM,
        out_shape=vmem((peers, 1, (ROWS // 2 + 1) * COLS), I32),
        compiler_params=PARAMS,
        cost_estimate=SMALL,
    )(owned, *map(in_vmem, (flux_e, back_e, flux_o, got)))


def add_kernel(got, out):
    half = ROWS // 2
    peers = got.shape[0] // (half + 1)
    m = lax.broadcasted_iota(I32, (1, COLS), 1)
    wanted = (lax.axis_index("z") * 4 + (m >> 5)) * 2 + lax.axis_index("c")
    wanted = (wanted * 4 + ((m >> 3) & 3)) * CO_DEV + (m & 7)
    head = got[pl.ds(half, peers, stride=half + 1), :]
    step = (head >> 8).astype(F32) * jnp.exp2((head & 255).astype(F32) - 128.0) * (2.0**-21)
    words = [got[pl.ds(r, peers, stride=half + 1), :] for r in range(half)]
    codes = [w >> 16 for w in words] + [(w << 16) >> 16 for w in words]
    chosen, pieces = [], []
    for r in range(ROWS):
        target = jnp.broadcast_to(head[:, r : r + 1], (peers, COLS))
        chosen.append(jnp.where(target == wanted, 1.0, 0.0))
        pieces.append(codes[r].astype(F32) * step[:, ROWS + r : ROWS + r + 1])
    chosen = jnp.concatenate(chosen, 0).T.astype(BF)
    sums = mm(chosen, jnp.concatenate(split(jnp.concatenate(pieces, 0)), 1))
    sums = sums[:, :COLS] + sums[:, COLS:]
    for d in range(out.shape[0]):
        out[d] = sums[d * CO_DEV : (d + 1) * CO_DEV]


def add_rows(arrived, peers):
    return pl.pallas_call(
        add_kernel,
        in_specs=[VM],
        out_specs=VM,
        out_shape=vmem((peers, CO_DEV, COLS), F32),
        compiler_params=PARAMS,
        cost_estimate=SOME,
    )(in_vmem(arrived))


def panel_kernel(back_o, up_in, low_in, up, low, panels, sem):
    odd = lax.axis_index("c") == 1
    tail = back_o[HALF * F :, :].astype(I32)
    for i in range(HALF):
        high, rest, power = (tail[3 * i + j : 3 * i + j + 1] for j in range(3))
        step = (high * 2048 + rest).astype(F32) * jnp.exp2(power.astype(F32)) * (2.0**-21)
        panels[i] = back_o[i * F : (i + 1) * F, :].astype(I32).astype(F32) * step

        @pl.when(odd)
        def _():
            pltpu.make_async_copy(panels.at[i], up.at[HALF + i], sem.at[i]).start()

        @pl.when(jnp.logical_not(odd))
        def _():
            pltpu.make_async_copy(panels.at[i], low.at[i], sem.at[i]).start()

    for i in range(HALF):
        pltpu.make_async_copy(panels.at[i], up.at[HALF + i], sem.at[i]).wait()


def put_panels(back_o, up, low):
    shape = pltpu.HBM((FC, F, COLS), F32)
    return pl.pallas_call(
        panel_kernel,
        in_specs=[VM] + [ANY] * 2,
        out_specs=[ANY] * 2,
        out_shape=[shape, shape],
        input_output_aliases={1: 0, 2: 1},
        scratch_shapes=[vmem((HALF, F, COLS), F32), pltpu.SemaphoreType.DMA((HALF,))],
        compiler_params=PARAMS,
        cost_estimate=SMALL,
    )(in_vmem(back_o), in_hbm(up), in_hbm(low))


def coarse_kernel(arrived, after, out):
    total = arrived[0]
    for d in range(1, arrived.shape[0]):
        total = total + arrived[d]
    out[...] = total


def sum_rows(arrived, after):
    return pl.pallas_call(
        coarse_kernel,
        in_specs=[VM, ANY],
        out_specs=VM,
        out_shape=jax.ShapeDtypeStruct((CO_DEV, COLS), F32),
        compiler_params=PARAMS,
        cost_estimate=SMALL,
    )(in_vmem(arrived), in_hbm(after))


def shards(schur_up, schur_low, resid_up, resid_low, counts, coarse_up, coarse_low):
    subs = lax.axis_size(SUB)
    s = lax.axis_index(SUB)
    odd = lax.axis_index("c").astype(I32)
    even = 1 - odd
    blocks = (schur_up, schur_low, resid_up, resid_low)

    (pack_a,) = pack([(0, EARLY, True, 0)], blocks)
    got_a = swapped(pack_a, True)
    *near, pack_b, owned = pack(
        [(k, 1, False, 1 if k == 0 else 0) for k in range(HALF)]
        + [(EARLY, HALF - EARLY, True, 2)],
        blocks,
        (counts, coarse_up, coarse_low),
        (pack_a,),
    )
    got_near = [swapped(value, False) for value in near]
    pack_b = passed_on(pack_b)
    got_b = swapped(pack_b, True)

    count = jnp.where(s < subs - 1, counts[0], 0)
    info = jnp.stack([odd, even, count])

    x_e, flux_e, theirs_e, own_m, own_r = solve_near(info, pack_b, blocks, got_near)
    back_e = swapped(x_e, False)
    back_flux = swapped(theirs_e, False)
    early = solve_far(own_m, own_r, got_a)
    x_o, code_o, flux_o = solve_last(info, own_m, own_r, got_b, *early, back_flux)
    back_o = swapped(code_o, True)

    near_axes, far_axes = ("z", "c"), ("y", "x")
    peers = lax.axis_size(near_axes)
    parcels = gather_rows(owned, flux_e, back_flux, flux_o, got_b, peers)
    arrived = lax.all_to_all(parcels, near_axes, 0, 0, tiled=True)
    sums = add_rows(arrived.reshape(peers * (ROWS // 2 + 1), COLS), lax.axis_size(far_axes))
    sums = lax.all_to_all(sums, far_axes, 0, 0, tiled=True)
    up, low = gather(x_e, back_e, x_o)
    up, low = put_panels(back_o, up, low)
    return (up, low, sum_rows(sums, up))


def solution(mesh):
    devices = mesh.devices.reshape(-1, 4, 2, mesh.shape["grp"])
    return jax.shard_map(
        shards,
        mesh=jax.sharding.Mesh(devices, ALL),
        in_specs=(
            P(ALL, None, None),
            P(ALL, None, None),
            P(ALL, None, None),
            P(ALL, None, None),
            P(ALL),
            P(ALL),
            P(ALL),
        ),
        out_specs=(
            P(ALL, None, None),
            P(ALL, None, None),
            P(ALL, None),
        ),
        check_vma=False,
    )
```

```python
import functools
import math

import jax
import jax.numpy as jnp
from jax import lax
from jax.experimental import pallas as pl
from jax.experimental.pallas import tpu as pltpu
from jax.sharding import PartitionSpec as P

F = 384
COLS = 128
WIDE = F + COLS
FC = 8
HALF = FC // 2
EARLY = 3
ITERS = 4
CO_DEV = 8
NOTE = 16
SUB = ("z", "y", "c")
ALL = (*SUB, "x")
ROWS = 4 * HALF
BF, F32, I32, I16 = jnp.bfloat16, jnp.float32, jnp.int32, jnp.int16

ANY = pl.BlockSpec(memory_space=pl.ANY)
VM = pl.BlockSpec(memory_space=pltpu.VMEM)
SM = pl.BlockSpec(memory_space=pltpu.SMEM)
PARAMS = pltpu.CompilerParams(vmem_limit_bytes=10 * 1024 * 1024)


def vmem(shape, dtype):
    return pltpu.VMEM(shape, dtype)


def in_vmem(value):
    return pltpu.with_memory_space_constraint(value, pltpu.VMEM)


def in_hbm(value):
    return pltpu.with_memory_space_constraint(value, pltpu.HBM)


def swapped(value, odd):
    size = lax.axis_size(SUB)
    pairs = []
    for i in range(size):
        j = ((i + 1) ^ 1) - 1 if odd else i ^ 1
        if 0 <= j < size:
            pairs.append((i, j))
    return lax.ppermute(value, SUB, pairs)


def pack_kernel(plans, *refs):
    su, sl, ru, rl = refs[:4]
    noted = any(plan[3] for plan in plans)
    outs, (*small, note, sem) = refs[-4 - len(plans) - noted : -4], refs[-4:]
    if noted:
        for i, (ref, kept_at) in enumerate(zip(refs[5:7], small)):
            pltpu.make_async_copy(ref, kept_at, sem.at[2, i]).start()
    odd = lax.axis_index("c") == 1
    jobs = []
    for out, (first, count, across, _) in zip(outs, plans):
        for j in range(count):
            jobs.append((out, j, first + j, odd if across else jnp.logical_not(odd)))

    def copies(slot, out, j, m, r, face):
        return (
            pltpu.make_async_copy(m.at[face], out.at[pl.ds(j * F, F), pl.ds(0, F)], sem.at[0, slot]),
            pltpu.make_async_copy(r.at[face], out.at[pl.ds(j * F, F), pl.ds(F, COLS)], sem.at[1, slot]),
        )

    for slot, (out, j, face, use_up) in enumerate(jobs):

        @pl.when(use_up)
        def _():
            for c in copies(slot, out, j, su, ru, HALF + face):
                c.start()

        @pl.when(jnp.logical_not(use_up))
        def _():
            for c in copies(slot, out, j, sl, rl, face):
                c.start()

    if noted:
        for i, (ref, kept_at) in enumerate(zip(refs[5:7], small)):
            pltpu.make_async_copy(ref, kept_at, sem.at[2, i]).wait()
        coarse_up, coarse_low = small
        target = jnp.where(odd, coarse_up[:, HALF:], coarse_low[:, :HALF])
        note[...] = jnp.zeros_like(note)
        note[0:1, :] = jnp.broadcast_to(refs[4][0].astype(F32), (1, WIDE))
        note[1:2, 3 * HALF : ROWS] = (target // 64).astype(F32)
        note[2:3, 3 * HALF : ROWS] = (target % 64).astype(F32)
        for out, plan in zip(outs, plans):
            for k in range(plan[3]):
                start = plan[1] * F + k * NOTE
                out[start : start + NOTE, :] = note[...].astype(BF)
        owned = outs[-1]
        s = (lax.axis_index("z") * 4 + lax.axis_index("y")) * 2 + lax.axis_index("c")
        alone = (s == 0) | (s == lax.axis_size(SUB) - 1)
        owned[...] = jnp.zeros_like(owned)
        parts = [
            jnp.where(odd, coarse_low[:, HALF:], coarse_up[:, :HALF]),
            jnp.where(odd, coarse_low[:, :HALF], coarse_up[:, HALF:]),
            jnp.where(odd, coarse_up[:, :HALF], coarse_low[:, HALF:]),
            jnp.broadcast_to(jnp.where(alone, -1, 0), (1, HALF)),
        ]
        for i, part in enumerate(parts):
            owned[:, i * HALF : (i + 1) * HALF] = part.astype(F32)
    for slot, (out, j, face, _) in enumerate(jobs):
        for c in copies(slot, out, j, su, ru, HALF + face):
            c.wait()


def pack(plans, blocks, small=(), after=()):
    shapes = [vmem((plan[1] * F + NOTE * plan[3], WIDE), BF) for plan in plans]
    if small:
        shapes.append(jax.ShapeDtypeStruct((1, COLS), F32))
    given = [small[0], *[in_hbm(v[None]) for v in small[1:]]] if small else []
    return pl.pallas_call(
        functools.partial(pack_kernel, plans),
        in_specs=[ANY] * 4 + [SM] * len(small[:1]) + [ANY] * (len(small[1:]) + len(after)),
        out_specs=[VM] * len(shapes),
        out_shape=shapes,
        scratch_shapes=[
            vmem((1, FC), I32),
            vmem((1, FC), I32),
            vmem((NOTE, WIDE), F32),
            pltpu.SemaphoreType.DMA((3, FC)),
        ],
        compiler_params=PARAMS,
        cost_estimate=SMALL,
    )(*[in_hbm(b) for b in blocks], *given, *after)


def split(value):
    high = value.astype(BF)
    return high, (value - high.astype(F32)).astype(BF)


def three(row):
    high, low = split(row)
    high, low = high.astype(F32), low.astype(F32)
    return high, low, row - high - low


def mm(a, b):
    return jnp.dot(a, b, preferred_element_type=F32)


def prepare(own_m, own_r, oth_m, oth_r):
    source = mm(own_m, own_r) + mm(oth_m, oth_r)
    own_f, oth_f = own_m.astype(F32), oth_m.astype(F32)
    sums = three(jnp.sum(own_f, axis=0, keepdims=True))
    sums += three(jnp.sum(oth_f, axis=0, keepdims=True))
    matrix = own_f + oth_f
    eye = lax.broadcasted_iota(I32, (128, 128), 0) == lax.broadcasted_iota(I32, (128, 128), 1)
    pivots, bands = [], []
    for b in range(F // 128):
        band = matrix[b * 128 : (b + 1) * 128]
        parts = [band[:, c * 128 : (c + 1) * 128] for c in range(F // 128)]
        pivots.append(jnp.sum(jnp.where(eye, parts[b], 0.0), axis=1, keepdims=True))
        parts[b] = jnp.where(eye, 0.0, parts[b])
        bands.append(jnp.concatenate(parts, 1))
    inverse = jnp.broadcast_to(1.0 / jnp.concatenate(pivots, 0), (F, COLS))
    high, low = split(jnp.concatenate(bands, 0))
    return source, inverse, high, low, sums


def sweep(x, state):
    source, inverse, high, low, _ = state
    x_h, x_l = split(x)
    wide = mm(high, jnp.concatenate([x_h, x_l], 1))
    return (source - (wide[:, :COLS] + wide[:, COLS:] + mm(low, x_h))) * inverse


def fluxes(x, own_r, oth_r, sums):
    line = lax.broadcasted_iota(I32, (16, F), 0)
    left = jnp.zeros((16, F), F32)
    for i, row in enumerate(sums):
        left = jnp.where(line == i, row, left)
    x_h, x_l = split(x)
    prod = mm(left.astype(BF), jnp.concatenate([own_r, oth_r, x_h, x_l], 1))[:8]
    moved = prod[:, 2 * COLS : 3 * COLS] + prod[:, 3 * COLS :]
    line = lax.broadcasted_iota(I32, (8, COLS), 0)
    scale = 1.0 / math.sqrt(F)
    own = jnp.where(line < 3, prod[:, :COLS] - moved, 0.0)
    oth = jnp.where((line >= 3) & (line < 6), prod[:, COLS : 2 * COLS] - moved, 0.0)
    return (
        jnp.sum(own, axis=0, keepdims=True) * scale,
        jnp.sum(oth, axis=0, keepdims=True) * scale,
    )


def solve_pair(own, others):
    states = [prepare(m, r, o[:, :F], o[:, F:]) for (m, r), o in zip(own, others)]
    xs = [s[0] * s[1] for s in states]
    for _ in range(ITERS):
        xs = [sweep(x, s) for x, s in zip(xs, states)]
    return [
        (x, *fluxes(x, r, o[:, F:], s[4])) for x, s, (_, r), o in zip(xs, states, own, others)
    ]


def keeper(su, sl, ru, rl, use_up, first, count, m, r, sem, row):
    def copies(i, sm, sr, face):
        return (
            pltpu.make_async_copy(sm.at[face], m.at[i], sem.at[row, i]),
            pltpu.make_async_copy(sr.at[face], r.at[i], sem.at[row + 1, i]),
        )

    def start(i):
        @pl.when(use_up)
        def _():
            for c in copies(i, su, ru, first + i):
                c.start()

        @pl.when(jnp.logical_not(use_up))
        def _():
            for c in copies(i, sl, rl, HALF + first + i):
                c.start()

    def wait(i):
        for c in copies(i, su, ru, first + i):
            c.wait()

    return start, wait


def count_of(lower, info, note):
    return jnp.where(lower, info[2].astype(F32), note.astype(F32)[:1])


def near_kernel(info, after, su, sl, ru, rl, *refs):
    got = refs[:HALF]
    x_out, flux_out, theirs_out, next_m, next_r, m, r, other, note, sem = refs[HALF:]
    use_up = info[1] == 1
    own_start, own_wait = keeper(su, sl, ru, rl, use_up, 0, HALF, m, r, sem, 0)
    next_start, next_wait = keeper(
        su, sl, ru, rl, jnp.logical_not(use_up), 0, HALF, next_m, next_r, sem, 3
    )

    def got_copy(i):
        return pltpu.make_async_copy(got[i].at[pl.ds(0, F)], other.at[i], sem.at[2, i])

    note_copy = pltpu.make_async_copy(got[0].at[pl.ds(F, NOTE)], note, sem.at[2, HALF])
    for i in range(HALF):
        own_start(i)
        got_copy(i).start()
        if i == 0:
            note_copy.start()
    flux_out[...] = jnp.zeros_like(flux_out)
    theirs_out[...] = jnp.zeros_like(theirs_out)
    base = jnp.where(use_up, 0, HALF)
    for start in range(0, HALF, 2):
        faces = (start, start + 1)
        for i in faces:
            own_wait(i)
            got_copy(i).wait()
        if start == 0:
            for i in range(HALF):
                next_start(i)
            note_copy.wait()
            count = count_of(use_up, info, note[:, :COLS])
        solved = solve_pair([(m[i], r[i]) for i in faces], [other[i] for i in faces])
        for i, (x, mine, theirs) in zip(faces, solved):
            live = (base + i).astype(F32) < count
            x_out[i * F : (i + 1) * F, :] = jnp.where(live, x, 0.0)
            flux_out[i : i + 1, :] = jnp.where(live, mine, 0.0)
            theirs_out[i : i + 1, :] = jnp.where(live, theirs, 0.0)
    for i in range(HALF):
        next_wait(i)


def steps_of(top):
    step = jnp.maximum(top, 1e-28) * (1.0 / 32767.0)
    power = jnp.clip(jnp.floor(jnp.log(step) * (1.0 / math.log(2.0))), -120.0, 120.0)
    unit = jnp.exp2(power)
    digits = jnp.round(step / unit * float(2**21))
    return digits, power, digits * unit * (2.0**-21)


def coded(value, step):
    return jnp.clip(jnp.round(value * (1.0 / step)), -32767.0, 32767.0).astype(I32)


def solve_all(first, count, m, r, got):
    out = []
    for start in range(0, count, 3):
        faces = range(start, min(start + 3, count))
        out += solve_pair(
            [(m[first + i], r[first + i]) for i in faces],
            [got[i * F : (i + 1) * F, :] for i in faces],
        )
    return out


def put_codes(x, ref, i, tail):
    digits, power, step = steps_of(jnp.max(jnp.abs(x), axis=0, keepdims=True))
    ref[i * F : (i + 1) * F, :] = coded(x, step).astype(I16)
    digits = digits.astype(I32)
    line = lax.broadcasted_iota(I32, tail.shape, 0)
    for j, row in enumerate((digits >> 11, digits & 2047, power.astype(I32))):
        tail = jnp.where(line == 3 * i + j, row, tail)
    return tail


def far_kernel(m, r, got, x_out, code_out, tail_out, flux_out):
    flux_out[...] = jnp.zeros_like(flux_out)
    tail = jnp.zeros((NOTE, COLS), I32)
    for i, (x, mine, theirs) in enumerate(solve_all(0, EARLY, m, r, got)):
        x_out[i * F : (i + 1) * F, :] = x
        tail = put_codes(x, code_out, i, tail)
        flux_out[i : i + 1, :] = mine
        flux_out[HALF + i : HALF + i + 1, :] = theirs
    tail_out[...] = tail


def last_kernel(
    info, m, r, got, x_in, code_in, tail_in, flux_in, after, x_out, code_out, flux_out
):
    late = HALF - EARLY
    use_up = info[0] == 1
    count = count_of(use_up, info, got[late * F : late * F + NOTE, :COLS])
    base = jnp.where(use_up, 0, HALF)
    code_out[: EARLY * F, :] = code_in[...]
    tail = tail_in[...]
    solved = [
        (x_in[k * F : (k + 1) * F, :], flux_in[k : k + 1, :], flux_in[HALF + k : HALF + k + 1, :])
        for k in range(EARLY)
    ]
    solved += solve_all(EARLY, late, m, r, got)
    line = lax.broadcasted_iota(I32, (NOTE, COLS), 0)
    for i, (x, mine, theirs) in enumerate(solved):
        live = (base + i).astype(F32) < count
        x_out[i * F : (i + 1) * F, :] = jnp.where(live, x, 0.0)
        if i >= EARLY:
            tail = put_codes(x, code_out, i, tail)
        dead = jnp.logical_not(live)
        tail = jnp.where((line >= 3 * i) & (line < 3 * i + 3) & dead, 0, tail)
        flux_out[i : i + 1, :] = jnp.where(live, mine, 0.0)
        flux_out[HALF + i : HALF + i + 1, :] = jnp.where(live, theirs, 0.0)
    code_out[HALF * F :, :] = tail.astype(I16)


def kept(count):
    return [vmem((count, F, F), BF), vmem((count, F, COLS), BF)]


SOME = pl.CostEstimate(flops=3*10**9, bytes_accessed=3*10**7, transcendentals=0)
SMALL = pl.CostEstimate(flops=1000, bytes_accessed=1000, transcendentals=0)


def passed_on(value):
    def kernel(value, out):
        out[...] = value[...]

    return pl.pallas_call(
        kernel,
        in_specs=[VM],
        out_specs=VM,
        out_shape=vmem(value.shape, value.dtype),
        compiler_params=PARAMS,
        cost_estimate=SOME,
    )(in_vmem(value))


def solve_near(info, after, blocks, got_near):
    return pl.pallas_call(
        near_kernel,
        in_specs=[SM] + [ANY] * (5 + HALF),
        out_specs=[VM] * 5,
        out_shape=[vmem((HALF * F, COLS), F32)] + [vmem((FC, COLS), F32)] * 2 + kept(HALF),
        scratch_shapes=[
            *kept(HALF),
            vmem((HALF, F, WIDE), BF),
            vmem((NOTE, WIDE), BF),
            pltpu.SemaphoreType.DMA((5, HALF + 1)),
        ],
        compiler_params=PARAMS,
        cost_estimate=SMALL,
    )(info, after, *[in_hbm(b) for b in (*blocks, *got_near)])


def solve_far(m, r, got):
    return pl.pallas_call(
        far_kernel,
        in_specs=[VM] * 3,
        out_specs=[VM] * 4,
        out_shape=[
            vmem((EARLY * F, COLS), F32),
            vmem((EARLY * F, COLS), I16),
            vmem((NOTE, COLS), I32),
            vmem((FC, COLS), F32),
        ],
        compiler_params=PARAMS,
        cost_estimate=SMALL,
    )(*map(in_vmem, (m, r, got)))


def solve_last(info, m, r, got, *early):
    return pl.pallas_call(
        last_kernel,
        in_specs=[SM] + [VM] * (3 + len(early)),
        out_specs=[VM] * 3,
        out_shape=[
            vmem((HALF * F, COLS), F32),
            vmem((HALF * F + NOTE, COLS), I16),
            vmem((FC, COLS), F32),
        ],
        compiler_params=PARAMS,
        cost_estimate=SMALL,
    )(info, *map(in_vmem, (m, r, got, *early)))


def place(ref, first, panels, sem, slot):
    out = []
    for i in range(HALF):
        c = pltpu.make_async_copy(panels.at[pl.ds(i * F, F)], ref.at[first + i], sem.at[slot, i])
        c.start()
        out.append(c)
    return out


def gather_kernel(x_e, back_e, x_o, up, low, sem):
    odd = lax.axis_index("c") == 1

    @pl.when(odd)
    def _():
        copies = place(low, HALF, x_e, sem, 0) + place(low, 0, back_e, sem, 1)
        copies += place(up, 0, x_o, sem, 2)
        for c in copies:
            c.wait()

    @pl.when(jnp.logical_not(odd))
    def _():
        copies = place(up, 0, x_e, sem, 0) + place(up, HALF, back_e, sem, 1)
        copies += place(low, HALF, x_o, sem, 2)
        for c in copies:
            c.wait()


def gather(x_e, back_e, x_o):
    shape = pltpu.HBM((FC, F, COLS), F32)
    return pl.pallas_call(
        gather_kernel,
        in_specs=[VM] * 3,
        out_specs=[ANY] * 2,
        out_shape=[shape, shape],
        scratch_shapes=[pltpu.SemaphoreType.DMA((3, HALF))],
        compiler_params=PARAMS,
        cost_estimate=SOME,
    )(x_e, back_e, x_o)


def gather_rows_kernel(owned, flux_e, back_e, flux_o, got, out):
    rows = jnp.concatenate([flux_e[:HALF], back_e[:HALF], flux_o[...]], 0)
    top = jnp.max(jnp.abs(rows), axis=1, keepdims=True)
    digits, power, step = steps_of(jnp.broadcast_to(top, rows.shape))
    codes = coded(rows, step)
    scales = digits.astype(I32) * 256 + (power.astype(I32) + 128)
    late = HALF - EARLY
    note = got[late * F : late * F + NOTE, :COLS].astype(F32)
    head = (owned[...] + note[1:2] * 64.0 + note[2:3]).astype(I32)
    lane = lax.broadcasted_iota(I32, (1, COLS), 1)
    for i in range(ROWS):
        head = jnp.where(lane == ROWS + i, scales[i : i + 1], head)
    half = ROWS // 2
    pairs = codes[:half] * 65536 + (codes[half:] & 65535)
    line = jnp.concatenate([pairs[i : i + 1] for i in range(half)] + [head], 1)
    for d in range(out.shape[0]):
        out[d] = line


def gather_rows(owned, flux_e, back_e, flux_o, got, peers):
    return pl.pallas_call(
        gather_rows_kernel,
        in_specs=[VM] * 5,
        out_specs=VM,
        out_shape=vmem((peers, 1, (ROWS // 2 + 1) * COLS), I32),
        compiler_params=PARAMS,
        cost_estimate=SMALL,
    )(owned, *map(in_vmem, (flux_e, back_e, flux_o, got)))


def add_kernel(got, out):
    half = ROWS // 2
    peers = got.shape[0] // (half + 1)
    m = lax.broadcasted_iota(I32, (1, COLS), 1)
    wanted = (lax.axis_index("z") * 4 + (m >> 5)) * 2 + lax.axis_index("c")
    wanted = (wanted * 4 + ((m >> 3) & 3)) * CO_DEV + (m & 7)
    head = got[pl.ds(half, peers, stride=half + 1), :]
    step = (head >> 8).astype(F32) * jnp.exp2((head & 255).astype(F32) - 128.0) * (2.0**-21)
    words = [got[pl.ds(r, peers, stride=half + 1), :] for r in range(half)]
    codes = [w >> 16 for w in words] + [(w << 16) >> 16 for w in words]
    chosen, pieces = [], []
    for r in range(ROWS):
        target = jnp.broadcast_to(head[:, r : r + 1], (peers, COLS))
        chosen.append(jnp.where(target == wanted, 1.0, 0.0))
        pieces.append(codes[r].astype(F32) * step[:, ROWS + r : ROWS + r + 1])
    chosen = jnp.concatenate(chosen, 0).T.astype(BF)
    sums = mm(chosen, jnp.concatenate(split(jnp.concatenate(pieces, 0)), 1))
    sums = sums[:, :COLS] + sums[:, COLS:]
    for d in range(out.shape[0]):
        out[d] = sums[d * CO_DEV : (d + 1) * CO_DEV]


def add_rows(arrived, peers):
    return pl.pallas_call(
        add_kernel,
        in_specs=[VM],
        out_specs=VM,
        out_shape=vmem((peers, CO_DEV, COLS), F32),
        compiler_params=PARAMS,
        cost_estimate=SOME,
    )(in_vmem(arrived))


def panel_kernel(back_o, up_in, low_in, up, low, panels, sem):
    odd = lax.axis_index("c") == 1
    tail = back_o[HALF * F :, :].astype(I32)
    for i in range(HALF):
        high, rest, power = (tail[3 * i + j : 3 * i + j + 1] for j in range(3))
        step = (high * 2048 + rest).astype(F32) * jnp.exp2(power.astype(F32)) * (2.0**-21)
        panels[i] = back_o[i * F : (i + 1) * F, :].astype(I32).astype(F32) * step

        @pl.when(odd)
        def _():
            pltpu.make_async_copy(panels.at[i], up.at[HALF + i], sem.at[i]).start()

        @pl.when(jnp.logical_not(odd))
        def _():
            pltpu.make_async_copy(panels.at[i], low.at[i], sem.at[i]).start()

    for i in range(HALF):
        pltpu.make_async_copy(panels.at[i], up.at[HALF + i], sem.at[i]).wait()


def put_panels(back_o, up, low):
    shape = pltpu.HBM((FC, F, COLS), F32)
    return pl.pallas_call(
        panel_kernel,
        in_specs=[VM] + [ANY] * 2,
        out_specs=[ANY] * 2,
        out_shape=[shape, shape],
        input_output_aliases={1: 0, 2: 1},
        scratch_shapes=[vmem((HALF, F, COLS), F32), pltpu.SemaphoreType.DMA((HALF,))],
        compiler_params=PARAMS,
        cost_estimate=SMALL,
    )(in_vmem(back_o), in_hbm(up), in_hbm(low))


def coarse_kernel(arrived, after, out):
    total = arrived[0]
    for d in range(1, arrived.shape[0]):
        total = total + arrived[d]
    out[...] = total


def sum_rows(arrived, after):
    return pl.pallas_call(
        coarse_kernel,
        in_specs=[VM, ANY],
        out_specs=VM,
        out_shape=jax.ShapeDtypeStruct((CO_DEV, COLS), F32),
        compiler_params=PARAMS,
        cost_estimate=SMALL,
    )(in_vmem(arrived), in_hbm(after))


def shards(schur_up, schur_low, resid_up, resid_low, counts, coarse_up, coarse_low):
    subs = lax.axis_size(SUB)
    s = lax.axis_index(SUB)
    odd = lax.axis_index("c").astype(I32)
    even = 1 - odd
    blocks = (schur_up, schur_low, resid_up, resid_low)

    (pack_a,) = pack([(0, EARLY, True, 0)], blocks)
    got_a = swapped(pack_a, True)
    *near, pack_b, owned = pack(
        [(k, 1, False, 1 if k == 0 else 0) for k in range(HALF)]
        + [(EARLY, HALF - EARLY, True, 1)],
        blocks,
        (counts, coarse_up, coarse_low),
        (pack_a,),
    )
    got_near = [swapped(value, False) for value in near]
    pack_b = passed_on(pack_b)
    got_b = swapped(pack_b, True)

    count = jnp.where(s < subs - 1, counts[0], 0)
    info = jnp.stack([odd, even, count])

    x_e, flux_e, theirs_e, own_m, own_r = solve_near(info, pack_b, blocks, got_near)
    back_e = swapped(x_e, False)
    back_flux = swapped(theirs_e, False)
    early = solve_far(own_m, own_r, got_a)
    x_o, code_o, flux_o = solve_last(info, own_m, own_r, got_b, *early, back_flux)
    back_o = swapped(code_o, True)

    near_axes, far_axes = ("z", "c"), ("y", "x")
    peers = lax.axis_size(near_axes)
    parcels = gather_rows(owned, flux_e, back_flux, flux_o, got_b, peers)
    arrived = lax.all_to_all(parcels, near_axes, 0, 0, tiled=True)
    sums = add_rows(arrived.reshape(peers * (ROWS // 2 + 1), COLS), lax.axis_size(far_axes))
    sums = lax.all_to_all(sums, far_axes, 0, 0, tiled=True)
    up, low = gather(x_e, back_e, x_o)
    up, low = put_panels(back_o, up, low)
    return (up, low, sum_rows(sums, up))


def solution(mesh):
    devices = mesh.devices.reshape(-1, 4, 2, mesh.shape["grp"])
    return jax.shard_map(
        shards,
        mesh=jax.sharding.Mesh(devices, ALL),
        in_specs=(
            P(ALL, None, None),
            P(ALL, None, None),
            P(ALL, None, None),
            P(ALL, None, None),
            P(ALL),
            P(ALL),
            P(ALL),
        ),
        out_specs=(
            P(ALL, None, None),
            P(ALL, None, None),
            P(ALL, None),
        ),
        check_vma=False,
    )
```

```python
import functools
import math

import jax
import jax.numpy as jnp
from jax import lax
from jax.experimental import pallas as pl
from jax.experimental.pallas import tpu as pltpu
from jax.sharding import PartitionSpec as P

F = 384
COLS = 128
WIDE = F + COLS
FC = 8
HALF = FC // 2
EARLY = 3
ITERS = 4
CO_DEV = 8
NOTE = 16
SUB = ("z", "y", "c")
ALL = (*SUB, "x")
ROWS = 4 * HALF
BF, F32, I32, I16 = jnp.bfloat16, jnp.float32, jnp.int32, jnp.int16

ANY = pl.BlockSpec(memory_space=pl.ANY)
VM = pl.BlockSpec(memory_space=pltpu.VMEM)
SM = pl.BlockSpec(memory_space=pltpu.SMEM)
PARAMS = pltpu.CompilerParams(vmem_limit_bytes=10 * 1024 * 1024)


def vmem(shape, dtype):
    return pltpu.VMEM(shape, dtype)


def in_vmem(value):
    return pltpu.with_memory_space_constraint(value, pltpu.VMEM)


def in_hbm(value):
    return pltpu.with_memory_space_constraint(value, pltpu.HBM)


def swapped(value, odd):
    size = lax.axis_size(SUB)
    pairs = []
    for i in range(size):
        j = ((i + 1) ^ 1) - 1 if odd else i ^ 1
        if 0 <= j < size:
            pairs.append((i, j))
    return lax.ppermute(value, SUB, pairs)


def pack_kernel(plans, *refs):
    su, sl, ru, rl = refs[:4]
    noted = any(plan[3] for plan in plans)
    outs, (*small, note, sem) = refs[-4 - len(plans) - noted : -4], refs[-4:]
    if noted:
        for i, (ref, kept_at) in enumerate(zip(refs[5:7], small)):
            pltpu.make_async_copy(ref, kept_at, sem.at[2, i]).start()
    odd = lax.axis_index("c") == 1
    jobs = []
    for out, (first, count, across, _) in zip(outs, plans):
        for j in range(count):
            jobs.append((out, j, first + j, odd if across else jnp.logical_not(odd)))

    def copies(slot, out, j, m, r, face):
        return (
            pltpu.make_async_copy(m.at[face], out.at[pl.ds(j * F, F), pl.ds(0, F)], sem.at[0, slot]),
            pltpu.make_async_copy(r.at[face], out.at[pl.ds(j * F, F), pl.ds(F, COLS)], sem.at[1, slot]),
        )

    for slot, (out, j, face, use_up) in enumerate(jobs):

        @pl.when(use_up)
        def _():
            for c in copies(slot, out, j, su, ru, HALF + face):
                c.start()

        @pl.when(jnp.logical_not(use_up))
        def _():
            for c in copies(slot, out, j, sl, rl, face):
                c.start()

    if noted:
        for i, (ref, kept_at) in enumerate(zip(refs[5:7], small)):
            pltpu.make_async_copy(ref, kept_at, sem.at[2, i]).wait()
        coarse_up, coarse_low = small
        target = jnp.where(odd, coarse_up[:, HALF:], coarse_low[:, :HALF])
        note[...] = jnp.zeros_like(note)
        note[0:1, :] = jnp.broadcast_to(refs[4][0].astype(F32), (1, WIDE))
        note[1:2, 3 * HALF : ROWS] = (target // 64).astype(F32)
        note[2:3, 3 * HALF : ROWS] = (target % 64).astype(F32)
        for out, plan in zip(outs, plans):
            for k in range(plan[3]):
                start = plan[1] * F + k * NOTE
                out[start : start + NOTE, :] = note[...].astype(BF)
        owned = outs[-1]
        s = (lax.axis_index("z") * 4 + lax.axis_index("y")) * 2 + lax.axis_index("c")
        alone = (s == 0) | (s == lax.axis_size(SUB) - 1)
        owned[...] = jnp.zeros_like(owned)
        parts = [
            jnp.where(odd, coarse_low[:, HALF:], coarse_up[:, :HALF]),
            jnp.where(odd, coarse_low[:, :HALF], coarse_up[:, HALF:]),
            jnp.where(odd, coarse_up[:, :HALF], coarse_low[:, HALF:]),
            jnp.broadcast_to(jnp.where(alone, -1, 0), (1, HALF)),
        ]
        for i, part in enumerate(parts):
            owned[:, i * HALF : (i + 1) * HALF] = part.astype(F32)
    for slot, (out, j, face, _) in enumerate(jobs):
        for c in copies(slot, out, j, su, ru, HALF + face):
            c.wait()


def pack(plans, blocks, small=(), after=()):
    shapes = [vmem((plan[1] * F + NOTE * plan[3], WIDE), BF) for plan in plans]
    if small:
        shapes.append(jax.ShapeDtypeStruct((1, COLS), F32))
    given = [small[0], *[in_hbm(v[None]) for v in small[1:]]] if small else []
    return pl.pallas_call(
        functools.partial(pack_kernel, plans),
        in_specs=[ANY] * 4 + [SM] * len(small[:1]) + [ANY] * (len(small[1:]) + len(after)),
        out_specs=[VM] * len(shapes),
        out_shape=shapes,
        scratch_shapes=[
            vmem((1, FC), I32),
            vmem((1, FC), I32),
            vmem((NOTE, WIDE), F32),
            pltpu.SemaphoreType.DMA((3, FC)),
        ],
        compiler_params=PARAMS,
        cost_estimate=SMALL,
    )(*[in_hbm(b) for b in blocks], *given, *after)


def split(value):
    high = value.astype(BF)
    return high, (value - high.astype(F32)).astype(BF)


def three(row):
    high, low = split(row)
    high, low = high.astype(F32), low.astype(F32)
    return high, low, row - high - low


def mm(a, b):
    return jnp.dot(a, b, preferred_element_type=F32)


def prepare(own_m, own_r, oth_m, oth_r):
    source = mm(own_m, own_r) + mm(oth_m, oth_r)
    own_f, oth_f = own_m.astype(F32), oth_m.astype(F32)
    sums = three(jnp.sum(own_f, axis=0, keepdims=True))
    sums += three(jnp.sum(oth_f, axis=0, keepdims=True))
    matrix = own_f + oth_f
    eye = lax.broadcasted_iota(I32, (128, 128), 0) == lax.broadcasted_iota(I32, (128, 128), 1)
    pivots, bands = [], []
    for b in range(F // 128):
        band = matrix[b * 128 : (b + 1) * 128]
        parts = [band[:, c * 128 : (c + 1) * 128] for c in range(F // 128)]
        pivots.append(jnp.sum(jnp.where(eye, parts[b], 0.0), axis=1, keepdims=True))
        parts[b] = jnp.where(eye, 0.0, parts[b])
        bands.append(jnp.concatenate(parts, 1))
    inverse = jnp.broadcast_to(1.0 / jnp.concatenate(pivots, 0), (F, COLS))
    high, low = split(jnp.concatenate(bands, 0))
    return source, inverse, high, low, sums


def sweep(x, state):
    source, inverse, high, low, _ = state
    x_h, x_l = split(x)
    wide = mm(high, jnp.concatenate([x_h, x_l], 1))
    return (source - (wide[:, :COLS] + wide[:, COLS:] + mm(low, x_h))) * inverse


def fluxes(x, own_r, oth_r, sums):
    line = lax.broadcasted_iota(I32, (16, F), 0)
    left = jnp.zeros((16, F), F32)
    for i, row in enumerate(sums):
        left = jnp.where(line == i, row, left)
    x_h, x_l = split(x)
    prod = mm(left.astype(BF), jnp.concatenate([own_r, oth_r, x_h, x_l], 1))[:8]
    moved = prod[:, 2 * COLS : 3 * COLS] + prod[:, 3 * COLS :]
    line = lax.broadcasted_iota(I32, (8, COLS), 0)
    scale = 1.0 / math.sqrt(F)
    own = jnp.where(line < 3, prod[:, :COLS] - moved, 0.0)
    oth = jnp.where((line >= 3) & (line < 6), prod[:, COLS : 2 * COLS] - moved, 0.0)
    return (
        jnp.sum(own, axis=0, keepdims=True) * scale,
        jnp.sum(oth, axis=0, keepdims=True) * scale,
    )


def solve_pair(own, others):
    states = [prepare(m, r, o[:, :F], o[:, F:]) for (m, r), o in zip(own, others)]
    xs = [s[0] * s[1] for s in states]
    for _ in range(ITERS):
        xs = [sweep(x, s) for x, s in zip(xs, states)]
    return [
        (x, *fluxes(x, r, o[:, F:], s[4])) for x, s, (_, r), o in zip(xs, states, own, others)
    ]


def keeper(su, sl, ru, rl, use_up, first, count, m, r, sem, row):
    def copies(i, sm, sr, face):
        return (
            pltpu.make_async_copy(sm.at[face], m.at[i], sem.at[row, i]),
            pltpu.make_async_copy(sr.at[face], r.at[i], sem.at[row + 1, i]),
        )

    def start(i):
        @pl.when(use_up)
        def _():
            for c in copies(i, su, ru, first + i):
                c.start()

        @pl.when(jnp.logical_not(use_up))
        def _():
            for c in copies(i, sl, rl, HALF + first + i):
                c.start()

    def wait(i):
        for c in copies(i, su, ru, first + i):
            c.wait()

    return start, wait


def count_of(lower, info, note):
    return jnp.where(lower, info[2].astype(F32), note.astype(F32)[:1])


def near_kernel(info, after, su, sl, ru, rl, *refs):
    got = refs[:HALF]
    x_out, flux_out, theirs_out, next_m, next_r, m, r, other, note, sem = refs[HALF:]
    use_up = info[1] == 1
    own_start, own_wait = keeper(su, sl, ru, rl, use_up, 0, HALF, m, r, sem, 0)
    next_start, next_wait = keeper(
        su, sl, ru, rl, jnp.logical_not(use_up), 0, HALF, next_m, next_r, sem, 3
    )

    def got_copy(i):
        return pltpu.make_async_copy(got[i].at[pl.ds(0, F)], other.at[i], sem.at[2, i])

    note_copy = pltpu.make_async_copy(got[0].at[pl.ds(F, NOTE)], note, sem.at[2, HALF])
    for i in range(HALF):
        own_start(i)
        got_copy(i).start()
        if i == 0:
            note_copy.start()
    flux_out[...] = jnp.zeros_like(flux_out)
    theirs_out[...] = jnp.zeros_like(theirs_out)
    base = jnp.where(use_up, 0, HALF)
    for start in range(0, HALF, 2):
        faces = (start, start + 1)
        for i in faces:
            own_wait(i)
            got_copy(i).wait()
        if start == 0:
            for i in range(HALF):
                next_start(i)
            note_copy.wait()
            count = count_of(use_up, info, note[:, :COLS])
        solved = solve_pair([(m[i], r[i]) for i in faces], [other[i] for i in faces])
        for i, (x, mine, theirs) in zip(faces, solved):
            live = (base + i).astype(F32) < count
            x_out[i * F : (i + 1) * F, :] = jnp.where(live, x, 0.0)
            flux_out[i : i + 1, :] = jnp.where(live, mine, 0.0)
            theirs_out[i : i + 1, :] = jnp.where(live, theirs, 0.0)
    for i in range(HALF):
        next_wait(i)


def steps_of(top):
    step = jnp.maximum(top, 1e-28) * (1.0 / 32767.0)
    power = jnp.clip(jnp.floor(jnp.log(step) * (1.0 / math.log(2.0))), -120.0, 120.0)
    unit = jnp.exp2(power)
    digits = jnp.round(step / unit * float(2**21))
    return digits, power, digits * unit * (2.0**-21)


def coded(value, step):
    return jnp.clip(jnp.round(value * (1.0 / step)), -32767.0, 32767.0).astype(I32)


def solve_all(first, count, m, r, got):
    out = []
    for start in range(0, count, 3):
        faces = range(start, min(start + 3, count))
        out += solve_pair(
            [(m[first + i], r[first + i]) for i in faces],
            [got[i * F : (i + 1) * F, :] for i in faces],
        )
    return out


def put_codes(x, ref, i, tail):
    digits, power, step = steps_of(jnp.max(jnp.abs(x), axis=0, keepdims=True))
    ref[i * F : (i + 1) * F, :] = coded(x, step).astype(I16)
    digits = digits.astype(I32)
    line = lax.broadcasted_iota(I32, tail.shape, 0)
    for j, row in enumerate((digits >> 11, digits & 2047, power.astype(I32))):
        tail = jnp.where(line == 3 * i + j, row, tail)
    return tail


def far_kernel(m, r, got, x_out, code_out, tail_out, flux_out):
    flux_out[...] = jnp.zeros_like(flux_out)
    tail = jnp.zeros((NOTE, COLS), I32)
    for i, (x, mine, theirs) in enumerate(solve_all(0, EARLY, m, r, got)):
        x_out[i * F : (i + 1) * F, :] = x
        tail = put_codes(x, code_out, i, tail)
        flux_out[i : i + 1, :] = mine
        flux_out[HALF + i : HALF + i + 1, :] = theirs
    tail_out[...] = tail


def last_kernel(
    info, m, r, got, x_in, code_in, tail_in, flux_in, after, x_out, code_out, flux_out
):
    late = HALF - EARLY
    use_up = info[0] == 1
    count = count_of(use_up, info, got[late * F : late * F + NOTE, :COLS])
    base = jnp.where(use_up, 0, HALF)
    code_out[: EARLY * F, :] = code_in[...]
    tail = tail_in[...]
    solved = [
        (x_in[k * F : (k + 1) * F, :], flux_in[k : k + 1, :], flux_in[HALF + k : HALF + k + 1, :])
        for k in range(EARLY)
    ]
    solved += solve_all(EARLY, late, m, r, got)
    line = lax.broadcasted_iota(I32, (NOTE, COLS), 0)
    for i, (x, mine, theirs) in enumerate(solved):
        live = (base + i).astype(F32) < count
        x_out[i * F : (i + 1) * F, :] = jnp.where(live, x, 0.0)
        if i >= EARLY:
            tail = put_codes(x, code_out, i, tail)
        dead = jnp.logical_not(live)
        tail = jnp.where((line >= 3 * i) & (line < 3 * i + 3) & dead, 0, tail)
        flux_out[i : i + 1, :] = jnp.where(live, mine, 0.0)
        flux_out[HALF + i : HALF + i + 1, :] = jnp.where(live, theirs, 0.0)
    code_out[HALF * F :, :] = tail.astype(I16)


def kept(count):
    return [vmem((count, F, F), BF), vmem((count, F, COLS), BF)]


SOME = pl.CostEstimate(flops=3*10**9, bytes_accessed=3*10**7, transcendentals=0)
SMALL = pl.CostEstimate(flops=1000, bytes_accessed=1000, transcendentals=0)


def passed_on(value):
    def kernel(value, out):
        out[...] = value[...]

    return pl.pallas_call(
        kernel,
        in_specs=[VM],
        out_specs=VM,
        out_shape=vmem(value.shape, value.dtype),
        compiler_params=PARAMS,
        cost_estimate=SOME,
    )(in_vmem(value))


def solve_near(info, after, blocks, got_near):
    return pl.pallas_call(
        near_kernel,
        in_specs=[SM] + [ANY] * (5 + HALF),
        out_specs=[VM] * 5,
        out_shape=[vmem((HALF * F, COLS), F32)] + [vmem((FC, COLS), F32)] * 2 + kept(HALF),
        scratch_shapes=[
            *kept(HALF),
            vmem((HALF, F, WIDE), BF),
            vmem((NOTE, WIDE), BF),
            pltpu.SemaphoreType.DMA((5, HALF + 1)),
        ],
        compiler_params=PARAMS,
        cost_estimate=SMALL,
    )(info, after, *[in_hbm(b) for b in (*blocks, *got_near)])


def solve_far(m, r, got):
    return pl.pallas_call(
        far_kernel,
        in_specs=[VM] * 3,
        out_specs=[VM] * 4,
        out_shape=[
            vmem((EARLY * F, COLS), F32),
            vmem((EARLY * F, COLS), I16),
            vmem((NOTE, COLS), I32),
            vmem((FC, COLS), F32),
        ],
        compiler_params=PARAMS,
        cost_estimate=SMALL,
    )(*map(in_vmem, (m, r, got)))


def solve_last(info, m, r, got, *early):
    return pl.pallas_call(
        last_kernel,
        in_specs=[SM] + [VM] * (3 + len(early)),
        out_specs=[VM] * 3,
        out_shape=[
            vmem((HALF * F, COLS), F32),
            vmem((HALF * F + NOTE, COLS), I16),
            vmem((FC, COLS), F32),
        ],
        compiler_params=PARAMS,
        cost_estimate=SMALL,
    )(info, *map(in_vmem, (m, r, got, *early)))


def place(ref, first, panels, sem, slot):
    out = []
    for i in range(HALF):
        c = pltpu.make_async_copy(panels.at[pl.ds(i * F, F)], ref.at[first + i], sem.at[slot, i])
        c.start()
        out.append(c)
    return out


def gather_kernel(x_e, back_e, x_o, up, low, sem):
    odd = lax.axis_index("c") == 1

    @pl.when(odd)
    def _():
        copies = place(low, HALF, x_e, sem, 0) + place(low, 0, back_e, sem, 1)
        copies += place(up, 0, x_o, sem, 2)
        for c in copies:
            c.wait()

    @pl.when(jnp.logical_not(odd))
    def _():
        copies = place(up, 0, x_e, sem, 0) + place(up, HALF, back_e, sem, 1)
        copies += place(low, HALF, x_o, sem, 2)
        for c in copies:
            c.wait()


def gather(x_e, back_e, x_o):
    shape = pltpu.HBM((FC, F, COLS), F32)
    return pl.pallas_call(
        gather_kernel,
        in_specs=[VM] * 3,
        out_specs=[ANY] * 2,
        out_shape=[shape, shape],
        scratch_shapes=[pltpu.SemaphoreType.DMA((3, HALF))],
        compiler_params=PARAMS,
        cost_estimate=SOME,
    )(x_e, back_e, x_o)


def gather_rows_kernel(owned, flux_e, back_e, flux_o, got, out):
    rows = jnp.concatenate([flux_e[:HALF], back_e[:HALF], flux_o[...]], 0)
    top = jnp.max(jnp.abs(rows), axis=1, keepdims=True)
    digits, power, step = steps_of(jnp.broadcast_to(top, rows.shape))
    codes = coded(rows, step)
    scales = digits.astype(I32) * 256 + (power.astype(I32) + 128)
    late = HALF - EARLY
    note = got[late * F : late * F + NOTE, :COLS].astype(F32)
    head = (owned[...] + note[1:2] * 64.0 + note[2:3]).astype(I32)
    lane = lax.broadcasted_iota(I32, (1, COLS), 1)
    for i in range(ROWS):
        head = jnp.where(lane == ROWS + i, scales[i : i + 1], head)
    half = ROWS // 2
    pairs = codes[:half] * 65536 + (codes[half:] & 65535)
    line = jnp.concatenate([pairs[i : i + 1] for i in range(half)] + [head], 1)
    for d in range(out.shape[0]):
        out[d] = line


def gather_rows(owned, flux_e, back_e, flux_o, got, peers):
    return pl.pallas_call(
        gather_rows_kernel,
        in_specs=[VM] * 5,
        out_specs=VM,
        out_shape=vmem((peers, 1, (ROWS // 2 + 1) * COLS), I32),
        compiler_params=PARAMS,
        cost_estimate=SMALL,
    )(owned, *map(in_vmem, (flux_e, back_e, flux_o, got)))


def add_kernel(got, out):
    half = ROWS // 2
    peers = got.shape[0] // (half + 1)
    m = lax.broadcasted_iota(I32, (1, COLS), 1)
    wanted = (lax.axis_index("z") * 4 + (m >> 5)) * 2 + lax.axis_index("c")
    wanted = (wanted * 4 + ((m >> 3) & 3)) * CO_DEV + (m & 7)
    head = got[pl.ds(half, peers, stride=half + 1), :]
    step = (head >> 8).astype(F32) * jnp.exp2((head & 255).astype(F32) - 128.0) * (2.0**-21)
    words = [got[pl.ds(r, peers, stride=half + 1), :] for r in range(half)]
    codes = [w >> 16 for w in words] + [(w << 16) >> 16 for w in words]
    chosen, pieces = [], []
    for r in range(ROWS):
        target = jnp.broadcast_to(head[:, r : r + 1], (peers, COLS))
        chosen.append(jnp.where(target == wanted, 1.0, 0.0))
        pieces.append(codes[r].astype(F32) * step[:, ROWS + r : ROWS + r + 1])
    chosen = jnp.concatenate(chosen, 0).astype(BF)
    parts = jnp.concatenate(split(jnp.concatenate(pieces, 0)), 1)
    sums = lax.dot_general(chosen, parts, (((0,), (0,)), ((), ())), preferred_element_type=F32)
    sums = sums[:, :COLS] + sums[:, COLS:]
    for d in range(out.shape[0]):
        out[d] = sums[d * CO_DEV : (d + 1) * CO_DEV]


def add_rows(arrived, peers):
    return pl.pallas_call(
        add_kernel,
        in_specs=[VM],
        out_specs=VM,
        out_shape=vmem((peers, CO_DEV, COLS), F32),
        compiler_params=PARAMS,
        cost_estimate=SOME,
    )(in_vmem(arrived))


def panel_kernel(back_o, up_in, low_in, up, low, panels, sem):
    odd = lax.axis_index("c") == 1
    tail = back_o[HALF * F :, :].astype(I32)
    for i in range(HALF):
        high, rest, power = (tail[3 * i + j : 3 * i + j + 1] for j in range(3))
        step = (high * 2048 + rest).astype(F32) * jnp.exp2(power.astype(F32)) * (2.0**-21)
        panels[i] = back_o[i * F : (i + 1) * F, :].astype(I32).astype(F32) * step

        @pl.when(odd)
        def _():
            pltpu.make_async_copy(panels.at[i], up.at[HALF + i], sem.at[i]).start()

        @pl.when(jnp.logical_not(odd))
        def _():
            pltpu.make_async_copy(panels.at[i], low.at[i], sem.at[i]).start()

    for i in range(HALF):
        pltpu.make_async_copy(panels.at[i], up.at[HALF + i], sem.at[i]).wait()


def put_panels(back_o, up, low):
    shape = pltpu.HBM((FC, F, COLS), F32)
    return pl.pallas_call(
        panel_kernel,
        in_specs=[VM] + [ANY] * 2,
        out_specs=[ANY] * 2,
        out_shape=[shape, shape],
        input_output_aliases={1: 0, 2: 1},
        scratch_shapes=[vmem((HALF, F, COLS), F32), pltpu.SemaphoreType.DMA((HALF,))],
        compiler_params=PARAMS,
        cost_estimate=SMALL,
    )(in_vmem(back_o), in_hbm(up), in_hbm(low))


def coarse_kernel(arrived, after, out):
    total = arrived[0]
    for d in range(1, arrived.shape[0]):
        total = total + arrived[d]
    out[...] = total


def sum_rows(arrived, after):
    return pl.pallas_call(
        coarse_kernel,
        in_specs=[VM, ANY],
        out_specs=VM,
        out_shape=jax.ShapeDtypeStruct((CO_DEV, COLS), F32),
        compiler_params=PARAMS,
        cost_estimate=SMALL,
    )(in_vmem(arrived), in_hbm(after))


def shards(schur_up, schur_low, resid_up, resid_low, counts, coarse_up, coarse_low):
    subs = lax.axis_size(SUB)
    s = lax.axis_index(SUB)
    odd = lax.axis_index("c").astype(I32)
    even = 1 - odd
    blocks = (schur_up, schur_low, resid_up, resid_low)

    (pack_a,) = pack([(0, EARLY, True, 0)], blocks)
    got_a = swapped(pack_a, True)
    *near, pack_b, owned = pack(
        [(k, 1, False, 1 if k == 0 else 0) for k in range(HALF)]
        + [(EARLY, HALF - EARLY, True, 1)],
        blocks,
        (counts, coarse_up, coarse_low),
        (pack_a,),
    )
    got_near = [swapped(value, False) for value in near]
    pack_b = passed_on(pack_b)
    got_b = swapped(pack_b, True)

    count = jnp.where(s < subs - 1, counts[0], 0)
    info = jnp.stack([odd, even, count])

    x_e, flux_e, theirs_e, own_m, own_r = solve_near(info, pack_b, blocks, got_near)
    back_e = swapped(x_e, False)
    back_flux = swapped(theirs_e, False)
    early = solve_far(own_m, own_r, got_a)
    x_o, code_o, flux_o = solve_last(info, own_m, own_r, got_b, *early, back_flux)
    back_o = swapped(code_o, True)

    near_axes, far_axes = ("z", "c"), ("y", "x")
    peers = lax.axis_size(near_axes)
    parcels = gather_rows(owned, flux_e, back_flux, flux_o, got_b, peers)
    arrived = lax.all_to_all(parcels, near_axes, 0, 0, tiled=True)
    sums = add_rows(arrived.reshape(peers * (ROWS // 2 + 1), COLS), lax.axis_size(far_axes))
    sums = lax.all_to_all(sums, far_axes, 0, 0, tiled=True)
    up, low = gather(x_e, back_e, x_o)
    up, low = put_panels(back_o, up, low)
    return (up, low, sum_rows(sums, up))


def solution(mesh):
    devices = mesh.devices.reshape(-1, 4, 2, mesh.shape["grp"])
    return jax.shard_map(
        shards,
        mesh=jax.sharding.Mesh(devices, ALL),
        in_specs=(
            P(ALL, None, None),
            P(ALL, None, None),
            P(ALL, None, None),
            P(ALL, None, None),
            P(ALL),
            P(ALL),
            P(ALL),
        ),
        out_specs=(
            P(ALL, None, None),
            P(ALL, None, None),
            P(ALL, None),
        ),
        check_vma=False,
    )
```
